512 devices in a mesh: wide: 32 (over y, x), narrow: 16 (over z, core).
Axes of the slice: x: 4, y: 8, z: 8, core: 2. Of those that a mesh axis runs over, the one named last changes fastest.
Arguments:
- feat_queries: bfloat16 [131072, 256], P(('wide', 'narrow')), may hold values from -6 to 6
- feat_keys: bfloat16 [131072, 256], P(('wide', 'narrow')), may hold values from -6 to 6
- values: bfloat16 [131072, 1024], P(('wide', 'narrow')), may hold values from -8 to 8
- window_queries: bfloat16 [131072, 1024], P(('wide', 'narrow')), may hold values from -150 to 150
- window_keys: bfloat16 [131072, 1024], P(('wide', 'narrow')), may hold values from -5 to 5
Outputs:
- mixed: bfloat16 [131072, 1024], P(('wide', 'narrow'))
The draws below stay inside these ranges and needn't reach their ends.
All inputs are finite; a program needn't handle non-finite values.
Results may differ from the reference program's by a relative error of at most 0.0004.
The reference program's roundings to bfloat16 on the way (of `a` and `probs`) count: a program that leaves them out, or rounds other values in their place, can miss the bound.
Values may be sent and summed in bfloat16 or wider, within the bound.
No kernel may reach another device: no remote copies, remote signals or barrier semaphores. Data moves between devices by JAX's collectives and lax.ppermute only.
A program may use at most 64 MiB of HBM per device.

```python
import jax
import jax.numpy as jnp
import numpy as np
from jax import lax

HEADS = 16
FEAT_DIM = 16
VDIM = 64
WHEAD = 64
WINDOW = 256
TOK_DEV = 256
SEQ = 131072


def shared_keys(key):
    return jnp.clip(jax.random.normal(jax.random.fold_in(key, 71), (SEQ, HEADS * WHEAD), jnp.float32), -5.0, 5.0)


def draw_window_keys(key, part):
    return shared_keys(key).astype(jnp.bfloat16)


def draw_window_queries(key, part):
    base = jnp.clip(jax.random.normal(jax.random.fold_in(key, 83), (SEQ, HEADS * WHEAD), jnp.float32), -5.0, 5.0)
    return base.astype(jnp.bfloat16)


def draw_values(key, part):
    channels = HEADS * VDIM
    steps = jax.random.normal(jax.random.fold_in(key, 131), (SEQ, channels), jnp.float32) * jnp.float32((1.0 / SEQ) ** 0.5)
    drift = jnp.cumsum(steps, 0)
    offset = jax.random.uniform(jax.random.fold_in(key, 137), (1, channels), jnp.float32, -1.0, 1.0)
    rough = jnp.clip(jax.random.normal(jax.random.fold_in(key, 139), (SEQ, channels), jnp.float32), -4.0, 4.0)
    level = offset + drift
    return jnp.clip(rough + level, -8.0, 8.0).astype(jnp.bfloat16)


def steps_of(stream_key, dims, pieces, low, high):
    loudness, own = 1.0, jax.random.fold_in(stream_key, 6)
    for axis_at, shards_of in pieces:
        steps = jnp.exp(jax.random.uniform(jax.random.fold_in(own, axis_at), (shards_of,), jnp.float32, low / len(pieces), high / len(pieces)))
        loudness = loudness * jnp.repeat(steps, dims[axis_at] // shards_of).reshape([-1 if axis == axis_at else 1 for axis in range(len(dims))])
    return loudness


def centred(rng, extent, scale, reach, pieces=(), kind=jnp.bfloat16):
    drawn = jax.random.normal(rng, extent, jnp.float32) * scale
    if len(pieces) > 0:
        drawn = steps_of(rng, extent, pieces, -0.22, 0.18) * drawn
    return jnp.clip(drawn, min=-reach, max=reach).astype(kind)


def setup_inputs(seed: int = 0) -> dict:
    key_of = jax.random.split(jax.random.key(seed), 6)
    return {
        "feat_queries": centred(key_of[0], (SEQ, HEADS * FEAT_DIM), 1.0, 6.0, ((0, 512),)),
        "feat_keys": centred(key_of[1], (SEQ, HEADS * FEAT_DIM), 1.0, 6.0, ((0, 512),)),
        "values": draw_values(jax.random.fold_in(key_of[5], 71), 0),
        "window_queries": draw_window_queries(jax.random.fold_in(key_of[5], 71), 0),
        "window_keys": draw_window_keys(jax.random.fold_in(key_of[5], 71), 0),
    }


def expand(x, heads):
    rows = x.shape[0]
    x = x.astype(jnp.float32).reshape(rows, heads, -1)
    width = x.shape[-1]
    first, second = np.triu_indices(width)
    weight = np.where(first == second, 1.0 / np.sqrt(2.0 * width), 1.0 / np.sqrt(1.0 * width))
    quad = x[..., first] * x[..., second] * jnp.asarray(weight, jnp.float32)
    ones = jnp.ones((rows, heads, 1), jnp.float32)
    return jnp.concatenate([ones, x / width ** 0.25, quad], -1).astype(jnp.bfloat16)

def layer_block(qf, kf, values, wq, wk, rim_keys, rim_values, start, prior_state, prior_norm):
    rows, heads, feats = qf.shape
    val3 = values.reshape(rows, heads, -1)
    scores = jnp.einsum('thf,shf->hts', qf, kf, preferred_element_type=jnp.float32)
    causal = lax.broadcasted_iota(jnp.int32, (rows, rows), 0) >= lax.broadcasted_iota(jnp.int32, (rows, rows), 1)
    scores = jnp.where(causal[None], scores, jnp.float32(0.0))
    intra_den = lax.optimization_barrier(jnp.sum(scores, -1))
    intra_num = jnp.einsum('hts,shv->thv', scores.astype(jnp.bfloat16), val3, preferred_element_type=jnp.float32)
    qwide = qf.astype(jnp.float32)
    cross_num = jnp.einsum('thf,fhv->thv', qwide, prior_state.reshape(feats, heads, -1), precision=lax.Precision.HIGHEST)
    cross_den = jnp.einsum('thf,fh->th', qwide, prior_norm, precision=lax.Precision.HIGHEST)
    linear = (intra_num + cross_num) / (intra_den.T + cross_den)[..., None]
    span = rim_keys.shape[0]
    keys3 = jnp.concatenate([rim_keys, wk], 0).reshape(span + rows, heads, -1)
    vals3 = jnp.concatenate([rim_values, values], 0).reshape(span + rows, heads, -1)
    query3 = wq.reshape(rows, heads, -1)
    logits = jnp.einsum('thd,shd->hts', query3, keys3, preferred_element_type=jnp.float32) / jnp.sqrt(jnp.float32(query3.shape[-1]))
    row = lax.broadcasted_iota(jnp.int32, (rows, span + rows), 0)
    col = lax.broadcasted_iota(jnp.int32, (rows, span + rows), 1)
    valid = (col > row) & (col <= row + span) & (col - span + start >= 0)
    logits = jnp.where(valid[None], logits, jnp.float32(-1e+30))
    peak = lax.optimization_barrier(jnp.max(logits, -1, keepdims=True))
    expo = jnp.where(valid[None], jnp.exp(logits - peak), jnp.float32(0.0))
    probs = (expo / lax.optimization_barrier(jnp.sum(expo, -1, keepdims=True))).astype(jnp.bfloat16)
    window = jnp.einsum('hts,shv->thv', probs, vals3, preferred_element_type=jnp.float32)
    mixed = (linear + window).reshape(rows, -1).astype(jnp.bfloat16)
    own_state = jnp.einsum('shf,shv->fhv', kf, val3, preferred_element_type=jnp.float32).reshape(feats, -1)
    own_norm = lax.optimization_barrier(jnp.sum(kf.astype(jnp.float32), 0)).T
    return (mixed, own_state, own_norm)

def reference(feat_queries, feat_keys, values, window_queries, window_keys):
    blocks = SEQ // TOK_DEV
    span = WINDOW

    def split(a):
        return a.reshape(blocks, TOK_DEV, a.shape[-1])

    def step(carry, inputs):
        state, norm, rim_keys, rim_values = carry
        index, fq, fk, vv, wq, wk = inputs
        qf = expand(fq, HEADS)
        kf = expand(fk, HEADS)
        start = (index * TOK_DEV).astype(jnp.int32)
        mixed, own_state, own_norm = layer_block(qf, kf, vv, wq, wk, rim_keys, rim_values, start, state, norm)
        carry = (state + own_state, norm + own_norm, wk[TOK_DEV - span:], vv[TOK_DEV - span:])
        return (carry, mixed)
    feats = 1 + FEAT_DIM + FEAT_DIM * (FEAT_DIM + 1) // 2
    init = (jnp.zeros((feats, HEADS * VDIM), jnp.float32), jnp.zeros((feats, HEADS), jnp.float32), jnp.zeros((span, HEADS * WHEAD), jnp.bfloat16), jnp.zeros((span, HEADS * VDIM), jnp.bfloat16))
    xs = (jnp.arange(blocks, dtype=jnp.int32), split(feat_queries), split(feat_keys), split(values), split(window_queries), split(window_keys))
    carry, mixed = lax.scan(step, init, xs)
    return mixed.reshape(SEQ, HEADS * VDIM)
```

```python
import jax
import jax.numpy as jnp
import numpy as np
from jax import lax
from jax.experimental import pallas as pl
from jax.experimental.pallas import tpu as pltpu
from jax.sharding import Mesh
from jax.sharding import PartitionSpec as P

HEADS = 16
PAIRS = HEADS // 2
DIM = 16
ROWS = 256
FEATS = 153
FROWS = 160
PIECES = 32
PAIR_ROWS = 160
PROWS = 20
PIECE = (PROWS // 4, 4, 128)
TAIL = slice(152, 160)
VALUES = HEADS * 64
LANES = 128
AXES = ("y", "x", "z", "c")
F32 = jnp.float32
BF16 = jnp.bfloat16
W_DIAG = np.float32(1.0 / np.sqrt(2.0 * DIM))
W_OFF = np.float32(1.0 / np.sqrt(1.0 * DIM))
SCALE = np.float32(1.0 / DIM**0.25)
NT = (((1,), (1,)), ((), ()))


def features(x):
    twice = jnp.concatenate([x, x], 0)
    quarter = twice * W_OFF
    parts = [x * SCALE, x * x * W_DIAG]
    for shift in range(1, 8):
        parts.append(x * quarter[shift : shift + DIM])
    parts.append(x[:8] * quarter[8:16])
    one = lax.broadcasted_iota(jnp.int32, (8, x.shape[1]), 0) == 0
    parts.append(jnp.where(one, F32(1.0), F32(0.0)))
    return jnp.concatenate(parts, 0)


def low_lanes(rows):
    return lax.broadcasted_iota(jnp.int32, (rows, LANES), 1) < 64


def state_kernel(core_ref, fk_hbm, v_hbm, out_ref, fk_ref, v_ref, kt_ref, sems):
    half = VALUES // 2
    copies = [pltpu.make_async_copy(fk_hbm, fk_ref, sems.at[0])]
    for i in range(2):
        lanes = pl.ds(i * half, half)
        copies.append(pltpu.make_async_copy(v_hbm.at[:, lanes], v_ref.at[:, lanes], sems.at[1 + i]))
    for copy in copies:
        copy.start()
    first = core_ref[0] * (PAIRS // 2)
    copies[0].wait()
    kt_ref[...] = fk_ref[...].astype(F32).T
    lane = lax.broadcasted_iota(jnp.int32, (FROWS, LANES), 1)
    low = lane < 64
    vlow = low_lanes(ROWS)
    zcols = jnp.zeros((FROWS, LANES), F32)
    copies[1].wait()
    copies[2].wait()
    for i in range(PAIRS):
        pair = lax.rem(first + i, PAIRS)
        x = kt_ref[pl.ds(pl.multiple_of(pair * 32, 32), 32), :]
        v = v_ref[:, pl.ds(pl.multiple_of(pair * LANES, LANES), LANES)]
        one = jnp.ones_like(v)
        fa = features(x[:DIM]).astype(BF16)
        fb = features(x[DIM:]).astype(BF16)
        sa = jnp.dot(fa, jnp.where(vlow, v, one), preferred_element_type=F32)
        sb = jnp.dot(fb, jnp.where(vlow, one, v), preferred_element_type=F32)
        out_ref[i, :FROWS] = jnp.where(low, sa, sb)
        z = jnp.where(low, sb, sa)
        zcols = jnp.where((lane == i) | (lane == 64 + i), z, zcols)
    zrows = zcols.T
    blank = jnp.zeros((8, 2 * LANES - FROWS), F32)
    row = lax.broadcasted_iota(jnp.int32, (8, LANES), 0)
    for i in range(PAIRS):
        tail = out_ref[i, TAIL]
        for at, src in ((1, 64 + i), (3, i)):
            z = jnp.concatenate([jnp.broadcast_to(zrows[src : src + 1], (8, FROWS)), blank], 1)
            tail = jnp.where(row == at, z[:, :LANES], tail)
            tail = jnp.where(row == at + 1, z[:, LANES:], tail)
        out_ref[i, TAIL] = tail


def inner_kernel(p_ref, out_ref):
    run = jnp.zeros((PROWS, LANES), F32)
    for k in range(PIECES):
        at = slice(PROWS * k, PROWS * (k + 1))
        out_ref[at] = run
        run = run + p_ref[at]


def spread_kernel(y_ref, inner_ref, py_ref, out_ref):
    y = y_ref[0]
    outer = jnp.zeros((PROWS, LANES), F32)
    for k in range(8):
        outer = outer + jnp.where(k < y, py_ref[PROWS * k : PROWS * (k + 1)], F32(0.0))
    twice = jnp.concatenate([outer, outer], 0)
    for k in range(PIECES // 2):
        at = slice(2 * PROWS * k, 2 * PROWS * (k + 1))
        out_ref[at] = inner_ref[at] + twice


def split3(x):
    hi = x.astype(BF16)
    rest = x - hi.astype(F32)
    mid = rest.astype(BF16)
    lo = (rest - mid.astype(F32)).astype(BF16)
    return hi, mid, lo


def norm_columns(tails):
    rows = []
    for tail in tails:
        for row in (1, 3):
            rows.append(jnp.concatenate([tail[row : row + 1], tail[row + 1 : row + 2]], 1))
    rows.append(jnp.zeros((LANES - HEADS, 2 * LANES), F32))
    return jnp.concatenate(rows, 0).T[:FROWS]


def cross(qfs, s, zcols, at):
    low, tlow = low_lanes(FROWS), low_lanes(ROWS)
    s = jnp.where(lax.broadcasted_iota(jnp.int32, s.shape, 0) < FEATS, s, F32(0.0))
    res = []
    for h in range(2):
        z = jnp.broadcast_to(zcols[:, at + h : at + h + 1], (FROWS, LANES))
        hi, mid, lo = split3(jnp.where(low, s, z) if h == 0 else jnp.where(low, z, s))
        big = jnp.dot(qfs[h], jnp.concatenate([hi, mid], 1), preferred_element_type=F32)
        res.append(big[:, :LANES] + (big[:, LANES:] + jnp.dot(qfs[h], lo, preferred_element_type=F32)))
    num = jnp.where(tlow, res[0], res[1])
    den = pltpu.roll(jnp.where(tlow, res[1], res[0]), 64, 1)
    return num, den


def intra_kernel(core_ref, fq_ref, fk_ref, v_ref, sib_ref, qf_hbm, num_hbm, den_hbm, qt_ref, kt_ref, qf_ref, num_ref, den_ref, sems):
    second = core_ref[0] == 1
    qt_ref[...] = fq_ref[...].astype(F32).T
    kt_ref[...] = fk_ref[...].astype(F32).T
    low = low_lanes(ROWS)
    causal = lax.broadcasted_iota(jnp.int32, (ROWS, ROWS), 0) >= lax.broadcasted_iota(
        jnp.int32, (ROWS, ROWS), 1
    )
    zcols = norm_columns([sib_ref[i, TAIL] for i in range(PAIRS)])
    zcols = jnp.where(second, zcols, F32(0.0))
    copies = []
    for quad in range(PAIRS // 2):
        dens, rounded, qfs = [], [], []
        for h in range(4 * quad, 4 * quad + 4):
            rows = slice(h * DIM, (h + 1) * DIM)
            qf = features(qt_ref[rows, :]).T.astype(BF16)
            kf = features(kt_ref[rows, :]).astype(BF16)
            qf_ref[h] = qf
            qfs.append(qf)
            a = jnp.dot(qf, kf, preferred_element_type=F32)
            a = jnp.where(causal, a, F32(0.0))
            dens.append(jnp.sum(a, -1, keepdims=True))
            rounded.append(a.astype(BF16))
        wide = slice(quad * 256, (quad + 1) * 256)
        nums = jnp.dot(jnp.concatenate(rounded, 0), v_ref[:, wide], preferred_element_type=F32)
        for p in range(2):
            pair = 2 * quad + p
            s = jnp.where(second, sib_ref[pair], F32(0.0))
            num, den = cross(qfs[2 * p : 2 * p + 2], s, zcols, 2 * pair)
            lanes = slice(pair * LANES, (pair + 1) * LANES)
            here = slice(p * LANES, (p + 1) * LANES)
            n0 = nums[2 * p * ROWS : (2 * p + 1) * ROWS, here]
            n1 = nums[(2 * p + 1) * ROWS : (2 * p + 2) * ROWS, here]
            num_ref[:, lanes] = num + jnp.where(low, n0, n1)
            den_ref[:, lanes] = den + jnp.where(low, dens[2 * p], dens[2 * p + 1])
        heads = pl.ds(4 * quad, 4)
        lanes = pl.ds(quad * 256, 256)
        for k, (src, dst) in enumerate(
            (
                (qf_ref.at[heads], qf_hbm.at[heads]),
                (num_ref.at[:, lanes], num_hbm.at[:, lanes]),
                (den_ref.at[:, lanes], den_hbm.at[:, lanes]),
            )
        ):
            copy = pltpu.make_async_copy(src, dst, sems.at[k, quad])
            copy.start()
            copies.append(copy)
    for copy in copies:
        copy.wait()


def window_kernel(start_ref, q_ref, k_ref, v_ref, hk_ref, hv_ref, out_hbm, out_ref, sems):
    half = ROWS // 2
    inside = start_ref[0] > 0
    r = lax.broadcasted_iota(jnp.int32, (4 * half, ROWS), 0) % half
    c = lax.broadcasted_iota(jnp.int32, (4 * half, ROWS), 1)
    masks = (
        ((c > r) & inside, (c <= r)[:, :half]),
        ((c > r)[:, :half] & inside, c <= r + half),
    )
    worst = F32(-1e30)
    head = lax.broadcasted_iota(jnp.int32, (half, 256), 1) // 64
    copies = []
    for quad in range(PAIRS // 2):
        lanes = slice(quad * 256, (quad + 1) * 256)
        for b in range(2):
            mine = slice(half * b, half * (b + 1))
            q = q_ref[mine, lanes] * BF16(0.125)
            hs = slice(half * b, ROWS)
            os = slice(0, half * (b + 1))
            qs = jnp.concatenate([jnp.where(head == h, q, jnp.zeros_like(q)) for h in range(4)], 0)
            lh = lax.dot_general(qs, hk_ref[hs, lanes], NT, preferred_element_type=F32)
            lo = lax.dot_general(qs, k_ref[os, lanes], NT, preferred_element_type=F32)
            lh = jnp.where(masks[b][0], lh, worst)
            lo = jnp.where(masks[b][1], lo, worst)
            peak = jnp.maximum(jnp.max(lh, -1, keepdims=True), jnp.max(lo, -1, keepdims=True))
            eh = jnp.exp(lh - peak)
            eo = jnp.exp(lo - peak)
            inv = F32(1.0) / (jnp.sum(eh, -1, keepdims=True) + jnp.sum(eo, -1, keepdims=True))
            ph = (eh * inv).astype(BF16)
            po = (eo * inv).astype(BF16)
            o = jnp.dot(ph, hv_ref[hs, lanes], preferred_element_type=F32) + jnp.dot(
                po, v_ref[os, lanes], preferred_element_type=F32
            )
            res = o[:half]
            for h in range(1, 4):
                res = jnp.where(head == h, o[h * half : (h + 1) * half], res)
            out_ref[mine, lanes] = res
        at = pl.ds(quad * 256, 256)
        copy = pltpu.make_async_copy(out_ref.at[:, at], out_hbm.at[:, at], sems.at[quad])
        copy.start()
        copies.append(copy)
    for copy in copies:
        copy.wait()


def final_kernel(core_ref, mine_ref, other_ref, qf_hbm, num_hbm, den_hbm, win_hbm, out_ref, qf_ref, num_ref, den_ref, win_ref, sems):
    first = core_ref[0] * (PAIRS // 2)
    half = PAIRS // 2
    copies = []
    for i in range(4):
        quad = lax.rem(core_ref[0] * 2 + i, 4)
        heads = pl.ds(4 * quad, 4)
        lanes = pl.ds(pl.multiple_of(quad * 256, 256), 256)
        group = []
        for k, (src, dst) in enumerate(
            (
                (qf_hbm.at[heads], qf_ref.at[heads]),
                (num_hbm.at[:, lanes], num_ref.at[:, lanes]),
                (den_hbm.at[:, lanes], den_ref.at[:, lanes]),
                (win_hbm.at[:, lanes], win_ref.at[:, lanes]),
            )
        ):
            copy = pltpu.make_async_copy(src, dst, sems.at[k, i])
            copy.start()
            group.append(copy)
        copies.append(group)
    refs = [mine_ref] * half + [other_ref] * half
    zcols = norm_columns([refs[i][i % half, TAIL] for i in range(PAIRS)])
    for i in range(PAIRS):
        if i % 2 == 0:
            for copy in copies[i // 2]:
                copy.wait()
        pair = lax.rem(first + i, PAIRS)
        lanes = pl.ds(pl.multiple_of(pair * LANES, LANES), LANES)
        qfs = [qf_ref[pair * 2], qf_ref[pair * 2 + 1]]
        num, den = cross(qfs, refs[i][i % half], zcols, 2 * i)
        linear = (num + num_ref[:, lanes]) / (den + den_ref[:, lanes])
        out_ref[:, lanes] = (linear + win_ref[:, lanes]).astype(BF16)


def spec(kind=pltpu.VMEM):
    return pl.BlockSpec(memory_space=kind)


def call(kernel, ins, outs, scratch, flops, moved, name):
    made = pl.pallas_call(
        kernel,
        out_shape=[pltpu.HBM(o.shape, o.dtype) if k == HB else o for o, k in outs],
        in_specs=[spec(k) for k in ins],
        out_specs=[spec(k) for _, k in outs],
        scratch_shapes=scratch,
        compiler_params=pltpu.CompilerParams(vmem_limit_bytes=40 * 2**20),
        cost_estimate=pl.CostEstimate(flops=flops, bytes_accessed=moved, transcendentals=0),
        name=name,
    )
    return lambda *arrays: made(
        *(pltpu.with_memory_space_constraint(a, k) if k == HB else a for a, k in zip(arrays, ins, strict=True))
    )


def shape(*dims, dtype=F32):
    return jax.ShapeDtypeStruct(dims, dtype)


SM, VM, HB = pltpu.SMEM, pltpu.VMEM, pltpu.HBM
TURNED = pltpu.VMEM((256, ROWS), F32)
WIDE = pltpu.VMEM((ROWS, VALUES), F32)
QF = (HEADS, ROWS, FROWS)


def own_state(core, fk, v):
    return call(
        state_kernel, [SM, HB, HB], [(shape(PAIRS, PAIR_ROWS, LANES), VM)],
        [pltpu.VMEM((ROWS, 256), BF16), pltpu.VMEM((ROWS, VALUES), BF16), TURNED, pltpu.SemaphoreType.DMA((3,))],
        10**9, 5 * 10**6, "state",
    )(core, fk, v)[0]


def inner(pieces):
    flat = shape(PIECES * PROWS, LANES)
    return call(inner_kernel, [VM], [(flat, VM)], [], 2 * 10**9, 10**6, "inner")(pieces.reshape(flat.shape))[0]


def spread(y, before, rows):
    return call(spread_kernel, [SM, VM, VM], [(shape(PIECES * PROWS, LANES), VM)], [], 10**6, 10**6, "spread")(
        y, before, rows.reshape(-1, LANES)
    )[0]


def intra(core, fq, fk, v, sib):
    wide = shape(ROWS, VALUES)
    return call(
        intra_kernel, [SM, VM, VM, VM, VM], [(shape(*QF, dtype=BF16), HB), (wide, HB), (wide, HB)],
        [TURNED, TURNED, pltpu.VMEM(QF, BF16), WIDE, WIDE, pltpu.SemaphoreType.DMA((3, 4))],
        2000000000, 16 * 10**6, "intra",
    )(core, fq, fk, v, sib)


def window(start, q, k, v, hk, hv):
    return call(
        window_kernel, [SM] + [VM] * 5, [(shape(ROWS, VALUES), HB)], [WIDE, pltpu.SemaphoreType.DMA((4,))],
        2 * 10**9, 16 * 10**6, "window",
    )(start, q, k, v, hk, hv)[0]


def final(core, mine, other, qf, num, den, win):
    return call(
        final_kernel, [SM, VM, VM] + [HB] * 4, [(shape(ROWS, VALUES, dtype=BF16), VM)],
        [pltpu.VMEM(QF, BF16), WIDE, WIDE, WIDE, pltpu.SemaphoreType.DMA((4, 4))], 2 * 10**9, 10**7, "final",
    )(core, mine, other, qf, num, den, win)[0]


def exchange(array, axes):
    return lax.all_to_all(array, axes, split_axis=0, concat_axis=0, tiled=True)


def swap(array):
    return lax.ppermute(array, "c", [(0, 1), (1, 0)])


def scalar(value):
    return jnp.asarray(value, jnp.int32).reshape(1)


def after(first, *arrays):
    return lax.optimization_barrier((first, *arrays))


def body(fq, fk, v, wq, wk):
    core = scalar(lax.axis_index("c"))
    start = scalar(lax.axis_index(AXES))
    state = own_state(core, fk, v)
    sib = swap(state)
    half = PAIRS // 2
    chip = (state[:half] + sib[half:]).reshape(PIECES, *PIECE)
    chip, fq, fk = after(chip, fq, fk)
    pieces = exchange(chip, ("x", "z"))
    qf, num, den = intra(core, fq, fk, v, sib)
    pieces, qf, num, den = after(pieces, qf, num, den)
    total = jnp.broadcast_to(jnp.sum(pieces, 0), (8, *PIECE))
    total, pieces, wk_out, v_out = after(total, pieces, wk, v)
    rows = exchange(total, "y")
    count = lax.axis_size(AXES)
    pairs = [(i, i + 1) for i in range(count - 1)]
    hk = lax.ppermute(wk_out, AXES, pairs)
    hv = lax.ppermute(v_out, AXES, pairs)
    before = inner(pieces)
    rows, before = after(rows, before)
    back = spread(scalar(lax.axis_index("y")), before, rows)
    back, wq = after(back.reshape(PIECES, *PIECE), wq)
    mine = exchange(back, ("x", "z"))
    win = window(start, wq, wk, v, hk, hv)
    mine, win = after(mine, win)
    mine = mine.reshape(half, PAIR_ROWS, LANES)
    other = swap(mine)
    return final(core, mine, other, qf, num, den, win)


def solution(mesh):
    finer = Mesh(mesh.devices.reshape(8, 4, 8, 2), AXES)
    placed = P(AXES, None)
    return jax.shard_map(
        body, mesh=finer, in_specs=(placed,) * 5, out_specs=placed, check_vma=False
    )
```

```python
import functools

import jax
import jax.numpy as jnp
import numpy as np
from jax import lax
from jax.experimental import pallas as pl
from jax.experimental.pallas import tpu as pltpu
from jax.sharding import Mesh
from jax.sharding import PartitionSpec as P

HEADS = 16
PAIRS = HEADS // 2
DIM = 16
ROWS = 256
QUADS = 4
FEATS = 153
FROWS = 160
PIECES = 32
PAIR_ROWS = 160
PROWS = 20
PIECE = (PROWS // 4, 4, 128)
TAIL = slice(152, 160)
VALUES = HEADS * 64
LANES = 128
AXES = ("y", "x", "z", "c")
F32 = jnp.float32
BF16 = jnp.bfloat16
W_DIAG = np.float32(1.0 / np.sqrt(2.0 * DIM))
W_OFF = np.float32(1.0 / np.sqrt(1.0 * DIM))
SCALE = np.float32(1.0 / DIM**0.25)
NT = (((1,), (1,)), ((), ()))


def features(x):
    twice = jnp.concatenate([x, x], 0)
    quarter = twice * W_OFF
    parts = [x * SCALE, x * x * W_DIAG]
    for shift in range(1, 8):
        parts.append(x * quarter[shift : shift + DIM])
    parts.append(x[:8] * quarter[8:16])
    one = lax.broadcasted_iota(jnp.int32, (8, x.shape[1]), 0) == 0
    parts.append(jnp.where(one, F32(1.0), F32(0.0)))
    return jnp.concatenate(parts, 0)


def low_lanes(rows):
    return lax.broadcasted_iota(jnp.int32, (rows, LANES), 1) < 64


def state_kernel(core_ref, fk_hbm, v_hbm, out_ref, fk_ref, v_ref, kt_ref, sems):
    half = VALUES // 2
    copies = [pltpu.make_async_copy(fk_hbm, fk_ref, sems.at[0])]
    for i in range(2):
        lanes = pl.ds(i * half, half)
        copies.append(pltpu.make_async_copy(v_hbm.at[:, lanes], v_ref.at[:, lanes], sems.at[1 + i]))
    for copy in copies:
        copy.start()
    first = core_ref[0] * (PAIRS // 2)
    copies[0].wait()
    kt_ref[...] = fk_ref[...].astype(F32).T
    lane = lax.broadcasted_iota(jnp.int32, (FROWS, LANES), 1)
    low = lane < 64
    vlow = low_lanes(ROWS)
    zcols = jnp.zeros((FROWS, LANES), F32)
    copies[1].wait()
    copies[2].wait()
    for i in range(PAIRS):
        pair = lax.rem(first + i, PAIRS)
        x = kt_ref[pl.ds(pl.multiple_of(pair * 32, 32), 32), :]
        v = v_ref[:, pl.ds(pl.multiple_of(pair * LANES, LANES), LANES)]
        one = jnp.ones_like(v)
        fa = features(x[:DIM]).astype(BF16)
        fb = features(x[DIM:]).astype(BF16)
        sa = jnp.dot(fa, jnp.where(vlow, v, one), preferred_element_type=F32)
        sb = jnp.dot(fb, jnp.where(vlow, one, v), preferred_element_type=F32)
        out_ref[i, :FROWS] = jnp.where(low, sa, sb)
        z = jnp.where(low, sb, sa)
        zcols = jnp.where((lane == i) | (lane == 64 + i), z, zcols)
    zrows = zcols.T
    blank = jnp.zeros((8, 2 * LANES - FROWS), F32)
    row = lax.broadcasted_iota(jnp.int32, (8, LANES), 0)
    for i in range(PAIRS):
        tail = out_ref[i, TAIL]
        for at, src in ((1, 64 + i), (3, i)):
            z = jnp.concatenate([jnp.broadcast_to(zrows[src : src + 1], (8, FROWS)), blank], 1)
            tail = jnp.where(row == at, z[:, :LANES], tail)
            tail = jnp.where(row == at + 1, z[:, LANES:], tail)
        out_ref[i, TAIL] = tail


def inner_kernel(p_ref, out_ref):
    run = jnp.zeros((PROWS, LANES), F32)
    for k in range(PIECES):
        at = slice(PROWS * k, PROWS * (k + 1))
        out_ref[at] = run
        run = run + p_ref[at]


def spread_kernel(y_ref, inner_ref, py_ref, out_ref):
    y = y_ref[0]
    outer = jnp.zeros((PROWS, LANES), F32)
    for k in range(8):
        outer = outer + jnp.where(k < y, py_ref[PROWS * k : PROWS * (k + 1)], F32(0.0))
    twice = jnp.concatenate([outer, outer], 0)
    for k in range(PIECES // 2):
        at = slice(2 * PROWS * k, 2 * PROWS * (k + 1))
        out_ref[at] = inner_ref[at] + twice


def split3(x):
    hi = x.astype(BF16)
    rest = x - hi.astype(F32)
    mid = rest.astype(BF16)
    lo = (rest - mid.astype(F32)).astype(BF16)
    return hi, mid, lo


def norm_columns(tails):
    rows = []
    for tail in tails:
        for row in (1, 3):
            rows.append(jnp.concatenate([tail[row : row + 1], tail[row + 1 : row + 2]], 1))
    rows.append(jnp.zeros((LANES - len(rows), 2 * LANES), F32))
    return jnp.concatenate(rows, 0).T[:FROWS]


def laid_out(w, slot):
    gap = jnp.zeros((32, w.shape[1]), w.dtype)
    return jnp.concatenate([w[:LANES]] + [gap] * slot + [w[LANES:]] + [gap] * (3 - slot), 0)


def cross(qfs, s, zcols, at, slot):
    low, tlow = low_lanes(FROWS), low_lanes(ROWS)
    s = jnp.where(lax.broadcasted_iota(jnp.int32, s.shape, 0) < FEATS, s, F32(0.0))
    res = []
    for h in range(2):
        z = jnp.broadcast_to(zcols[:, at + h : at + h + 1], (FROWS, LANES))
        parts = split3(jnp.where(low, s, z) if h == 0 else jnp.where(low, z, s))
        hi, mid, lo = (laid_out(part, slot + h) for part in parts)
        big = jnp.dot(qfs[h], jnp.concatenate([hi, mid], 1), preferred_element_type=F32)
        res.append(big[:, :LANES] + (big[:, LANES:] + jnp.dot(qfs[h], lo, preferred_element_type=F32)))
    return jnp.where(tlow, res[0], res[1]), jnp.where(tlow, res[1], res[0])


def intra_kernel(core_ref, fq_ref, fk_ref, v_ref, sib_ref, qf_hbm, num_hbm, den_hbm, qt_ref, kt_ref, qf_ref, num_ref, den_ref, sems):
    second = core_ref[0] == 1
    qt_ref[...] = fq_ref[...].astype(F32).T
    kt_ref[...] = fk_ref[...].astype(F32).T
    low = low_lanes(ROWS)
    lane = lax.broadcasted_iota(jnp.int32, (ROWS, LANES), 1)
    causal = lax.broadcasted_iota(jnp.int32, (ROWS, ROWS), 0) >= lax.broadcasted_iota(
        jnp.int32, (ROWS, ROWS), 1
    )
    zcols = norm_columns([sib_ref[i, TAIL] for i in range(PAIRS)])
    zcols = jnp.where(second, zcols, F32(0.0))
    all_dens = jnp.zeros((ROWS, LANES), F32)
    copies = []

    def send(src, dst, k, quad):
        copy = pltpu.make_async_copy(src, dst, sems.at[k, quad])
        copy.start()
        copies.append(copy)

    for quad in range(QUADS):
        dens, rounded, mains, rests = [], [], [], []
        for h in range(4 * quad, 4 * quad + 4):
            f = features(qt_ref[h * DIM : (h + 1) * DIM, :])
            main = f[:LANES].T.astype(BF16)
            qf_ref[h] = main
            mains.append(main)
            rests.append(f[LANES:])
        rest = jnp.concatenate(rests, 0).T.astype(BF16)
        qf_ref[HEADS + quad] = rest
        qfs = [jnp.concatenate([main, rest], 1) for main in mains]
        for slot in range(4):
            h = 4 * quad + slot
            kf = laid_out(features(kt_ref[h * DIM : (h + 1) * DIM, :]).astype(BF16), slot)
            a = jnp.dot(qfs[slot], kf, preferred_element_type=F32)
            a = jnp.where(causal, a, F32(0.0))
            dens.append(jnp.sum(a, -1, keepdims=True))
            rounded.append(a.astype(BF16))
        wide = slice(quad * 256, (quad + 1) * 256)
        nums = jnp.dot(jnp.concatenate(rounded, 0), v_ref[:, wide], preferred_element_type=F32)
        for p in range(2):
            pair = 2 * quad + p
            s = jnp.where(second, sib_ref[pair], F32(0.0))
            num, den = cross(qfs[2 * p : 2 * p + 2], s, zcols, 2 * pair, 2 * p)
            here = slice(p * LANES, (p + 1) * LANES)
            n0 = nums[2 * p * ROWS : (2 * p + 1) * ROWS, here]
            n1 = nums[(2 * p + 1) * ROWS : (2 * p + 2) * ROWS, here]
            num_ref[quad, :, here] = num + jnp.where(low, n0, n1)
            den = den + jnp.where(low, dens[2 * p + 1], dens[2 * p])
            place = jnp.where(second, (pair + PAIRS // 2) % PAIRS, pair)
            all_dens = jnp.where(lane % 64 == place, den, all_dens)
        heads = pl.ds(4 * quad, 4)
        send(qf_ref.at[heads], qf_hbm.at[heads], 0, quad)
        send(qf_ref.at[pl.ds(HEADS + quad, 1)], qf_hbm.at[pl.ds(HEADS + quad, 1)], 1, quad)
        send(num_ref.at[quad], num_hbm.at[quad], 2, quad)
    den_ref[...] = all_dens
    send(den_ref, den_hbm, 3, 0)
    for copy in copies:
        copy.wait()


def window_kernel(start_ref, q_ref, k_ref, v_ref, hk_ref, hv_ref, out_hbm, out_ref, sems):
    half = ROWS // 2
    inside = start_ref[0] > 0
    r = lax.broadcasted_iota(jnp.int32, (4 * half, ROWS), 0) % half
    c = lax.broadcasted_iota(jnp.int32, (4 * half, ROWS), 1)
    masks = (
        ((c > r) & inside, (c <= r)[:, :half]),
        ((c > r)[:, :half] & inside, c <= r + half),
    )
    worst = F32(-1e30)
    head = lax.broadcasted_iota(jnp.int32, (half, 256), 1) // 64
    copies = []
    for quad in range(PAIRS // 2):
        lanes = slice(quad * 256, (quad + 1) * 256)
        for b in range(2):
            mine = slice(half * b, half * (b + 1))
            q = q_ref[mine, lanes] * BF16(0.125)
            hs = slice(half * b, ROWS)
            os = slice(0, half * (b + 1))
            qs = jnp.concatenate([jnp.where(head == h, q, jnp.zeros_like(q)) for h in range(4)], 0)
            lh = lax.dot_general(qs, hk_ref[hs, lanes], NT, preferred_element_type=F32)
            lo = lax.dot_general(qs, k_ref[os, lanes], NT, preferred_element_type=F32)
            lh = jnp.where(masks[b][0], lh, worst)
            lo = jnp.where(masks[b][1], lo, worst)
            peak = jnp.maximum(jnp.max(lh, -1, keepdims=True), jnp.max(lo, -1, keepdims=True))
            eh = jnp.exp(lh - peak)
            eo = jnp.exp(lo - peak)
            inv = F32(1.0) / (jnp.sum(eh, -1, keepdims=True) + jnp.sum(eo, -1, keepdims=True))
            ph = (eh * inv).astype(BF16)
            po = (eo * inv).astype(BF16)
            o = jnp.dot(ph, hv_ref[hs, lanes], preferred_element_type=F32) + jnp.dot(
                po, v_ref[os, lanes], preferred_element_type=F32
            )
            res = o[:half]
            for h in range(1, 4):
                res = jnp.where(head == h, o[h * half : (h + 1) * half], res)
            out_ref[quad, mine] = res
        copy = pltpu.make_async_copy(out_ref.at[quad], out_hbm.at[quad], sems.at[quad])
        copy.start()
        copies.append(copy)
    for copy in copies:
        copy.wait()


def finish(part, p_ref, qf_ref, num_ref, den_ref, win_ref, out_ref, q, zcols):
    low = low_lanes(ROWS)
    rest = qf_ref[8 + q]
    for p in range(2):
        i = 2 * q + p
        qfs = [jnp.concatenate([qf_ref[2 * i + h], rest], 1) for h in range(2)]
        num, den = cross(qfs, p_ref[i], zcols, 2 * i, 2 * p)
        at = PAIRS // 2 * part + i
        den = den + jnp.where(low, den_ref[:, at : at + 1], den_ref[:, 64 + at : 65 + at])
        here = slice(p * LANES, (p + 1) * LANES)
        linear = (num + num_ref[q, :, here]) / pltpu.roll(den, 64, 1)
        out_ref[q, :, here] = (linear + win_ref[q, :, here]).astype(BF16)


def norms_of(p_ref):
    return norm_columns([p_ref[i, TAIL] for i in range(PAIRS // 2)])


def leave(out_ref, out_hbm, half, q, sems):
    lanes = pl.ds(pl.multiple_of(half * 512 + q * 256, 256), 256)
    copy = pltpu.make_async_copy(out_ref.at[q], out_hbm.at[:, lanes], sems.at[q])
    copy.start()
    return copy


def first_kernel(
    core_ref, p_ref, qf_hbm, num_hbm, den_hbm, win_hbm, out_hbm, qf2_ref, num2_ref, den_ref, win2_ref,
    qf_ref, num_ref, win_ref, out_ref, sems, out_sems,
):
    core = core_ref[0]
    dens = pltpu.make_async_copy(den_hbm, den_ref, sems.at[2, 0])
    dens.start()
    groups = []
    for part, half in ((0, core), (1, 1 - core)):
        to = ((qf_ref, num_ref, win_ref), (qf2_ref, num2_ref, win2_ref))[part]
        two = pl.ds(2 * half, 2)
        group = []
        for k, (src, dst) in enumerate(
            (
                (qf_hbm.at[pl.ds(8 * half, 8)], to[0].at[pl.ds(0, 8)]),
                (qf_hbm.at[pl.ds(HEADS + 2 * half, 2)], to[0].at[pl.ds(8, 2)]),
                (num_hbm.at[two], to[1]),
                (win_hbm.at[two], to[2]),
            )
        ):
            copy = pltpu.make_async_copy(src, dst, sems.at[part, k])
            copy.start()
            group.append(copy)
        groups.append(group)
    zcols = norms_of(p_ref)
    dens.wait()
    for copy in groups[0]:
        copy.wait()
    leaving = []
    for q in range(2):
        finish(0, p_ref, qf_ref, num_ref, den_ref, win_ref, out_ref, q, zcols)
        leaving.append(leave(out_ref, out_hbm, core, q, out_sems))
    for copy in groups[1] + leaving:
        copy.wait()


def second_kernel(core_ref, p_ref, qf_ref, num_ref, den_ref, win_ref, done_hbm, out_hbm, out_ref, out_sems):
    zcols = norms_of(p_ref)
    leaving = []
    for q in range(2):
        finish(1, p_ref, qf_ref, num_ref, den_ref, win_ref, out_ref, q, zcols)
        leaving.append(leave(out_ref, out_hbm, 1 - core_ref[0], q, out_sems))
    for copy in leaving:
        copy.wait()


def spec(kind=pltpu.VMEM):
    return pl.BlockSpec(memory_space=kind)


def call(kernel, ins, outs, scratch, flops, moved, name, aliases={}):
    made = pl.pallas_call(
        kernel,
        out_shape=[pltpu.HBM(o.shape, o.dtype) if k == HB else o for o, k in outs],
        in_specs=[spec(k) for k in ins],
        out_specs=[spec(k) for _, k in outs],
        scratch_shapes=scratch,
        input_output_aliases=aliases,
        compiler_params=pltpu.CompilerParams(vmem_limit_bytes=40 * 2**20),
        cost_estimate=pl.CostEstimate(flops=flops, bytes_accessed=moved, transcendentals=0),
        name=name,
    )
    return lambda *arrays: made(
        *(pltpu.with_memory_space_constraint(a, k) if k == HB else a for a, k in zip(arrays, ins, strict=True))
    )


def shape(*dims, dtype=F32):
    return jax.ShapeDtypeStruct(dims, dtype)


SM, VM, HB = pltpu.SMEM, pltpu.VMEM, pltpu.HBM
TURNED = pltpu.VMEM((256, ROWS), F32)
WIDE = pltpu.VMEM((QUADS, ROWS, 256), F32)
QF = (HEADS + QUADS, ROWS, LANES)
DENS = (ROWS, LANES)
BY_QUADS = (QUADS, ROWS, 256)
HALF_QF = (10, ROWS, LANES)
HALF = (2, ROWS, 256)


def own_state(core, fk, v):
    return call(
        state_kernel, [SM, HB, HB], [(shape(PAIRS, PAIR_ROWS, LANES), VM)],
        [pltpu.VMEM((ROWS, 256), BF16), pltpu.VMEM((ROWS, VALUES), BF16), TURNED, pltpu.SemaphoreType.DMA((3,))],
        10**9, 5 * 10**6, "state",
    )(core, fk, v)[0]


def inner(pieces):
    flat = shape(PIECES * PROWS, LANES)
    return call(inner_kernel, [VM], [(flat, VM)], [], 2 * 10**9, 10**6, "inner")(pieces.reshape(flat.shape))[0]


def spread(y, before, rows):
    return call(spread_kernel, [SM, VM, VM], [(shape(PIECES * PROWS, LANES), VM)], [], 10**6, 10**6, "spread")(
        y, before, rows.reshape(-1, LANES)
    )[0]


def intra(core, fq, fk, v, sib):
    return call(
        intra_kernel, [SM, VM, VM, VM, VM],
        [(shape(*QF, dtype=BF16), HB), (shape(*BY_QUADS), HB), (shape(*DENS), HB)],
        [TURNED, TURNED, pltpu.VMEM(QF, BF16), WIDE, pltpu.VMEM(DENS, F32), pltpu.SemaphoreType.DMA((4, 4))],
        2 * 10**9, 16 * 10**6, "intra",
    )(core, fq, fk, v, sib)


def window(start, q, k, v, hk, hv):
    return call(
        window_kernel, [SM] + [VM] * 5, [(shape(*BY_QUADS), HB)], [WIDE, pltpu.SemaphoreType.DMA((4,))],
        2 * 10**9, 16 * 10**6, "window",
    )(start, q, k, v, hk, hv)[0]


OUT = (shape(ROWS, VALUES, dtype=BF16), HB)
OUT_SCRATCH = [pltpu.VMEM(HALF, BF16), pltpu.SemaphoreType.DMA((2,))]


def final_first(core, prior, qf, num, den, win):
    return call(
        first_kernel, [SM, VM] + [HB] * 4,
        [OUT, (shape(*HALF_QF, dtype=BF16), VM), (shape(*HALF), VM), (shape(*DENS), VM), (shape(*HALF), VM)],
        [pltpu.VMEM(HALF_QF, BF16), pltpu.VMEM(HALF, F32), pltpu.VMEM(HALF, F32), OUT_SCRATCH[0],
         pltpu.SemaphoreType.DMA((3, 4)), OUT_SCRATCH[1]],
        2 * 10**9, 10**7, "first",
    )(core, prior, qf, num, den, win)


def final_second(core, prior, qf, num, den, win, done):
    return call(
        second_kernel, [SM] + [VM] * 5 + [HB], [OUT], OUT_SCRATCH, 2 * 10**9, 10**6, "second", {6: 0}
    )(core, prior, qf, num, den, win, done)[0]


def exchange(array, axes):
    return lax.all_to_all(array, axes, split_axis=0, concat_axis=0, tiled=True)


def swap(array):
    return lax.ppermute(array, "c", [(0, 1), (1, 0)])


def scalar(value):
    return jnp.asarray(value, jnp.int32).reshape(1)


def after(first, *arrays):
    return lax.optimization_barrier((first, *arrays))


def body(fq, fk, v, wq, wk):
    core = scalar(lax.axis_index("c"))
    start = scalar(lax.axis_index(AXES))
    state = own_state(core, fk, v)
    sib = swap(state)
    half = PAIRS // 2
    chip = (state[:half] + sib[half:]).reshape(PIECES, *PIECE)
    chip, fq, fk = after(chip, fq, fk)
    pieces = exchange(chip, ("x", "z"))
    qf, num, den = intra(core, fq, fk, v, sib)
    count = lax.axis_size(AXES)
    pairs = [(i, i + 1) for i in range(count - 1)]
    qf, wk_out, v_out = after(qf, wk, v)
    hk = lax.ppermute(wk_out, AXES, pairs)
    hv = lax.ppermute(v_out, AXES, pairs)
    pieces, qf, num, den = after(pieces, qf, num, den)
    total = jnp.broadcast_to(jnp.sum(pieces, 0), (8, *PIECE))
    total, pieces = after(total, pieces)
    rows = exchange(total, "y")
    before = inner(pieces)
    rows, before = after(rows, before)
    back = spread(scalar(lax.axis_index("y")), before, rows)
    back, wq = after(back.reshape(PIECES, *PIECE), wq)
    mine = exchange(back, ("x", "z"))
    win = window(start, wq, wk, v, hk, hv)
    mine, win = after(mine, win)
    mine = mine.reshape(half, PAIR_ROWS, LANES)
    other = swap(mine)
    done, *rest = final_first(core, mine, qf, num, den, win)
    return final_second(core, other, *rest, done)


def solution(mesh):
    finer = Mesh(mesh.devices.reshape(8, 4, 8, 2), AXES)
    placed = P(AXES, None)
    return jax.shard_map(
        body, mesh=finer, in_specs=(placed,) * 5, out_specs=placed, check_vma=False
    )
```

```python
import functools

import jax
import jax.numpy as jnp
import numpy as np
from jax import lax
from jax.experimental import pallas as pl
from jax.experimental.pallas import tpu as pltpu
from jax.sharding import Mesh
from jax.sharding import PartitionSpec as P

HEADS = 16
PAIRS = HEADS // 2
DIM = 16
ROWS = 256
QUADS = 4
FEATS = 153
FROWS = 160
PIECES = 32
PAIR_ROWS = 160
PROWS = 20
PIECE = (PROWS // 4, 4, 128)
TAIL = slice(152, 160)
VALUES = HEADS * 64
LANES = 128
AXES = ("y", "x", "z", "c")
F32 = jnp.float32
BF16 = jnp.bfloat16
W_DIAG = np.float32(1.0 / np.sqrt(2.0 * DIM))
W_OFF = np.float32(1.0 / np.sqrt(1.0 * DIM))
SCALE = np.float32(1.0 / DIM**0.25)
NT = (((1,), (1,)), ((), ()))


def features(x):
    twice = jnp.concatenate([x, x], 0)
    quarter = twice * W_OFF
    parts = [x * SCALE, x * x * W_DIAG]
    for shift in range(1, 8):
        parts.append(x * quarter[shift : shift + DIM])
    parts.append(x[:8] * quarter[8:16])
    one = lax.broadcasted_iota(jnp.int32, (8, x.shape[1]), 0) == 0
    parts.append(jnp.where(one, F32(1.0), F32(0.0)))
    return jnp.concatenate(parts, 0)


def low_lanes(rows):
    return lax.broadcasted_iota(jnp.int32, (rows, LANES), 1) < 64


def state_kernel(core_ref, fk_hbm, v_hbm, out_ref, fk_ref, v_ref, kt_ref, sems):
    half = VALUES // 2
    copies = [pltpu.make_async_copy(fk_hbm, fk_ref, sems.at[0])]
    for i in range(2):
        lanes = pl.ds(i * half, half)
        copies.append(pltpu.make_async_copy(v_hbm.at[:, lanes], v_ref.at[:, lanes], sems.at[1 + i]))
    for copy in copies:
        copy.start()
    first = core_ref[0] * (PAIRS // 2)
    copies[0].wait()
    kt_ref[...] = fk_ref[...].astype(F32).T
    lane = lax.broadcasted_iota(jnp.int32, (FROWS, LANES), 1)
    low = lane < 64
    vlow = low_lanes(ROWS)
    zcols = jnp.zeros((FROWS, LANES), F32)
    copies[1].wait()
    copies[2].wait()
    for i in range(PAIRS):
        pair = lax.rem(first + i, PAIRS)
        x = kt_ref[pl.ds(pl.multiple_of(pair * 32, 32), 32), :]
        v = v_ref[:, pl.ds(pl.multiple_of(pair * LANES, LANES), LANES)]
        one = jnp.ones_like(v)
        fa = features(x[:DIM]).astype(BF16)
        fb = features(x[DIM:]).astype(BF16)
        sa = jnp.dot(fa, jnp.where(vlow, v, one), preferred_element_type=F32)
        sb = jnp.dot(fb, jnp.where(vlow, one, v), preferred_element_type=F32)
        out_ref[i, :FROWS] = jnp.where(low, sa, sb)
        z = jnp.where(low, sb, sa)
        zcols = jnp.where((lane == i) | (lane == 64 + i), z, zcols)
    zrows = zcols.T
    blank = jnp.zeros((8, 2 * LANES - FROWS), F32)
    row = lax.broadcasted_iota(jnp.int32, (8, LANES), 0)
    for i in range(PAIRS):
        tail = out_ref[i, TAIL]
        for at, src in ((1, 64 + i), (3, i)):
            z = jnp.concatenate([jnp.broadcast_to(zrows[src : src + 1], (8, FROWS)), blank], 1)
            tail = jnp.where(row == at, z[:, :LANES], tail)
            tail = jnp.where(row == at + 1, z[:, LANES:], tail)
        out_ref[i, TAIL] = tail


def inner_kernel(p_ref, out_ref):
    run = jnp.zeros((PROWS, LANES), F32)
    for k in range(PIECES):
        at = slice(PROWS * k, PROWS * (k + 1))
        out_ref[at] = run
        run = run + p_ref[at]


def spread_kernel(y_ref, inner_ref, py_ref, out_ref):
    y = y_ref[0]
    outer = jnp.zeros((PROWS, LANES), F32)
    for k in range(8):
        outer = outer + jnp.where(k < y, py_ref[PROWS * k : PROWS * (k + 1)], F32(0.0))
    twice = jnp.concatenate([outer, outer], 0)
    for k in range(PIECES // 2):
        at = slice(2 * PROWS * k, 2 * PROWS * (k + 1))
        out_ref[at] = inner_ref[at] + twice


def split3(x):
    hi = x.astype(BF16)
    rest = x - hi.astype(F32)
    mid = rest.astype(BF16)
    lo = (rest - mid.astype(F32)).astype(BF16)
    return hi, mid, lo


def norm_columns(tails):
    rows = []
    for tail in tails:
        for row in (1, 3):
            rows.append(jnp.concatenate([tail[row : row + 1], tail[row + 1 : row + 2]], 1))
    rows.append(jnp.zeros((LANES - len(rows), 2 * LANES), F32))
    return jnp.concatenate(rows, 0).T[:FROWS]


def laid_out(w, slot):
    gap = jnp.zeros((32, w.shape[1]), w.dtype)
    return jnp.concatenate([w[:LANES]] + [gap] * slot + [w[LANES:]] + [gap] * (3 - slot), 0)


def cross(qfs, s, zcols, at, slot):
    low, tlow = low_lanes(FROWS), low_lanes(ROWS)
    s = jnp.where(lax.broadcasted_iota(jnp.int32, s.shape, 0) < FEATS, s, F32(0.0))
    res = []
    for h in range(2):
        z = jnp.broadcast_to(zcols[:, at + h : at + h + 1], (FROWS, LANES))
        parts = split3(jnp.where(low, s, z) if h == 0 else jnp.where(low, z, s))
        hi, mid, lo = (laid_out(part, slot + h) for part in parts)
        big = jnp.dot(qfs[h], jnp.concatenate([hi, mid], 1), preferred_element_type=F32)
        res.append(big[:, :LANES] + (big[:, LANES:] + jnp.dot(qfs[h], lo, preferred_element_type=F32)))
    return jnp.where(tlow, res[0], res[1]), jnp.where(tlow, res[1], res[0])


def intra_kernel(core_ref, fq_ref, fk_ref, v_ref, sib_ref, qf_hbm, num_hbm, den_hbm, qt_ref, kt_ref, qf_ref, num_ref, den_ref, sems):
    second = core_ref[0] == 1
    qt_ref[...] = fq_ref[...].astype(F32).T
    kt_ref[...] = fk_ref[...].astype(F32).T
    low = low_lanes(ROWS)
    lane = lax.broadcasted_iota(jnp.int32, (ROWS, LANES), 1)
    causal = lax.broadcasted_iota(jnp.int32, (ROWS, ROWS), 0) >= lax.broadcasted_iota(
        jnp.int32, (ROWS, ROWS), 1
    )
    zcols = norm_columns([sib_ref[i, TAIL] for i in range(PAIRS)])
    zcols = jnp.where(second, zcols, F32(0.0))
    all_dens = jnp.zeros((ROWS, LANES), F32)
    copies = []

    def send(src, dst, k, quad):
        copy = pltpu.make_async_copy(src, dst, sems.at[k, quad])
        copy.start()
        copies.append(copy)

    for quad in range(QUADS):
        dens, rounded, mains, rests = [], [], [], []
        for h in range(4 * quad, 4 * quad + 4):
            f = features(qt_ref[h * DIM : (h + 1) * DIM, :])
            main = f[:LANES].T.astype(BF16)
            qf_ref[h] = main
            mains.append(main)
            rests.append(f[LANES:])
        rest = jnp.concatenate(rests, 0).T.astype(BF16)
        qf_ref[HEADS + quad] = rest
        qfs = [jnp.concatenate([main, rest], 1) for main in mains]
        for slot in range(4):
            h = 4 * quad + slot
            kf = laid_out(features(kt_ref[h * DIM : (h + 1) * DIM, :]).astype(BF16), slot)
            a = jnp.dot(qfs[slot], kf, preferred_element_type=F32)
            a = jnp.where(causal, a, F32(0.0))
            dens.append(jnp.sum(a, -1, keepdims=True))
            rounded.append(a.astype(BF16))
        wide = slice(quad * 256, (quad + 1) * 256)
        nums = jnp.dot(jnp.concatenate(rounded, 0), v_ref[:, wide], preferred_element_type=F32)
        for p in range(2):
            pair = 2 * quad + p
            s = jnp.where(second, sib_ref[pair], F32(0.0))
            num, den = cross(qfs[2 * p : 2 * p + 2], s, zcols, 2 * pair, 2 * p)
            here = slice(p * LANES, (p + 1) * LANES)
            n0 = nums[2 * p * ROWS : (2 * p + 1) * ROWS, here]
            n1 = nums[(2 * p + 1) * ROWS : (2 * p + 2) * ROWS, here]
            num_ref[quad, :, here] = num + jnp.where(low, n0, n1)
            den = den + jnp.where(low, dens[2 * p + 1], dens[2 * p])
            place = jnp.where(second, (pair + PAIRS // 2) % PAIRS, pair)
            all_dens = jnp.where(lane % 64 == place, den, all_dens)
        heads = pl.ds(4 * quad, 4)
        send(qf_ref.at[heads], qf_hbm.at[heads], 0, quad)
        send(qf_ref.at[pl.ds(HEADS + quad, 1)], qf_hbm.at[pl.ds(HEADS + quad, 1)], 1, quad)
        send(num_ref.at[quad], num_hbm.at[quad], 2, quad)
    den_ref[...] = all_dens
    send(den_ref, den_hbm, 3, 0)
    for copy in copies:
        copy.wait()


def window_kernel(start_ref, q_ref, k_ref, v_ref, hk_ref, hv_ref, out_hbm, out_ref, sems):
    half = ROWS // 2
    inside = start_ref[0] > 0
    r = lax.broadcasted_iota(jnp.int32, (4 * half, ROWS), 0) % half
    c = lax.broadcasted_iota(jnp.int32, (4 * half, ROWS), 1)
    masks = (
        ((c > r) & inside, (c <= r)[:, :half]),
        ((c > r)[:, :half] & inside, c <= r + half),
    )
    worst = F32(-1e30)
    head = lax.broadcasted_iota(jnp.int32, (half, 256), 1) // 64
    copies = []
    for quad in range(PAIRS // 2):
        lanes = slice(quad * 256, (quad + 1) * 256)
        for b in range(2):
            mine = slice(half * b, half * (b + 1))
            q = q_ref[mine, lanes] * BF16(0.125)
            hs = slice(half * b, ROWS)
            os = slice(0, half * (b + 1))
            qs = jnp.concatenate([jnp.where(head == h, q, jnp.zeros_like(q)) for h in range(4)], 0)
            lh = lax.dot_general(qs, hk_ref[hs, lanes], NT, preferred_element_type=F32)
            lo = lax.dot_general(qs, k_ref[os, lanes], NT, preferred_element_type=F32)
            lh = jnp.where(masks[b][0], lh, worst)
            lo = jnp.where(masks[b][1], lo, worst)
            peak = jnp.maximum(jnp.max(lh, -1, keepdims=True), jnp.max(lo, -1, keepdims=True))
            eh = jnp.exp(lh - peak)
            eo = jnp.exp(lo - peak)
            inv = F32(1.0) / (jnp.sum(eh, -1, keepdims=True) + jnp.sum(eo, -1, keepdims=True))
            ph = (eh * inv).astype(BF16)
            po = (eo * inv).astype(BF16)
            o = jnp.dot(ph, hv_ref[hs, lanes], preferred_element_type=F32) + jnp.dot(
                po, v_ref[os, lanes], preferred_element_type=F32
            )
            res = o[:half]
            for h in range(1, 4):
                res = jnp.where(head == h, o[h * half : (h + 1) * half], res)
            out_ref[quad, mine] = res
        copy = pltpu.make_async_copy(out_ref.at[quad], out_hbm.at[quad], sems.at[quad])
        copy.start()
        copies.append(copy)
    for copy in copies:
        copy.wait()


def finish(part, p_ref, qf_ref, num_ref, den_ref, win_ref, out_ref, q, zcols):
    low = low_lanes(ROWS)
    rest = qf_ref[8 + q]
    for p in range(2):
        i = 2 * q + p
        qfs = [jnp.concatenate([qf_ref[2 * i + h], rest], 1) for h in range(2)]
        num, den = cross(qfs, p_ref[i], zcols, 2 * i, 2 * p)
        at = PAIRS // 2 * part + i
        den = den + jnp.where(low, den_ref[:, at : at + 1], den_ref[:, 64 + at : 65 + at])
        here = slice(p * LANES, (p + 1) * LANES)
        linear = (num + num_ref[q, :, here]) / pltpu.roll(den, 64, 1)
        out_ref[q, :, here] = (linear + win_ref[q, :, here]).astype(BF16)


def norms_of(p_ref):
    return norm_columns([p_ref[i, TAIL] for i in range(PAIRS // 2)])


def leave(out_ref, out_hbm, half, q, sems):
    lanes = pl.ds(pl.multiple_of(half * 512 + q * 256, 256), 256)
    copy = pltpu.make_async_copy(out_ref.at[q], out_hbm.at[:, lanes], sems.at[q])
    copy.start()
    return copy


def stage_kernel(core_ref, qf_hbm, num_hbm, den_hbm, win_hbm, *refs):
    core = core_ref[0]
    qf_ref, num_ref, win_ref, qf2_ref, num2_ref, den_ref, sems = refs
    copies = []
    for k, (src, dst) in enumerate(
        (
            (den_hbm, den_ref),
            (qf_hbm.at[pl.ds(8 * core, 8)], qf_ref.at[pl.ds(0, 8)]),
            (qf_hbm.at[pl.ds(HEADS + 2 * core, 2)], qf_ref.at[pl.ds(8, 2)]),
            (num_hbm.at[pl.ds(2 * core, 2)], num_ref),
            (qf_hbm.at[pl.ds(8 - 8 * core, 8)], qf2_ref.at[pl.ds(0, 8)]),
            (qf_hbm.at[pl.ds(HEADS + 2 - 2 * core, 2)], qf2_ref.at[pl.ds(8, 2)]),
            (num_hbm.at[pl.ds(2 - 2 * core, 2)], num2_ref),
            (win_hbm.at[pl.ds(2 * core, 2)], win_ref),
        )
    ):
        copies.append(pltpu.make_async_copy(src, dst, sems.at[k]))
    for copy in copies:
        copy.start()
    for copy in copies:
        copy.wait()


def first_kernel(core_ref, p_ref, qf_ref, num_ref, den_ref, win_ref, win_hbm, out_ref, win2_ref, sem):
    win = pltpu.make_async_copy(win_hbm.at[pl.ds(2 - 2 * core_ref[0], 2)], win2_ref, sem.at[0])
    win.start()
    zcols = norms_of(p_ref)
    for q in range(2):
        finish(0, p_ref, qf_ref, num_ref, den_ref, win_ref, out_ref, q, zcols)
    win.wait()


def second_kernel(core_ref, p_ref, qf_ref, num_ref, den_ref, win_ref, done_ref, out_hbm, out_ref, sems):
    core = core_ref[0]
    leaving = [leave(done_ref, out_hbm, core, q, sems.at[0]) for q in range(2)]
    zcols = norms_of(p_ref)
    for q in range(2):
        finish(1, p_ref, qf_ref, num_ref, den_ref, win_ref, out_ref, q, zcols)
        leaving.append(leave(out_ref, out_hbm, 1 - core, q, sems.at[1]))
    for copy in leaving:
        copy.wait()


def spec(kind=pltpu.VMEM):
    return pl.BlockSpec(memory_space=kind)


def call(kernel, ins, outs, scratch, flops, moved, name):
    made = pl.pallas_call(
        kernel,
        out_shape=[pltpu.HBM(o.shape, o.dtype) if k == HB else o for o, k in outs],
        in_specs=[spec(k) for k in ins],
        out_specs=[spec(k) for _, k in outs],
        scratch_shapes=scratch,
        compiler_params=pltpu.CompilerParams(vmem_limit_bytes=40 * 2**20),
        cost_estimate=pl.CostEstimate(flops=flops, bytes_accessed=moved, transcendentals=0),
        name=name,
    )
    return lambda *arrays: made(
        *(pltpu.with_memory_space_constraint(a, k) if k == HB else a for a, k in zip(arrays, ins, strict=True))
    )


def shape(*dims, dtype=F32):
    return jax.ShapeDtypeStruct(dims, dtype)


SM, VM, HB = pltpu.SMEM, pltpu.VMEM, pltpu.HBM
TURNED = pltpu.VMEM((256, ROWS), F32)
WIDE = pltpu.VMEM((QUADS, ROWS, 256), F32)
QF = (HEADS + QUADS, ROWS, LANES)
DENS = (ROWS, LANES)
BY_QUADS = (QUADS, ROWS, 256)
HALF_QF = (10, ROWS, LANES)
HALF = (2, ROWS, 256)


def own_state(core, fk, v):
    return call(
        state_kernel, [SM, HB, HB], [(shape(PAIRS, PAIR_ROWS, LANES), VM)],
        [pltpu.VMEM((ROWS, 256), BF16), pltpu.VMEM((ROWS, VALUES), BF16), TURNED, pltpu.SemaphoreType.DMA((3,))],
        10**9, 5 * 10**6, "state",
    )(core, fk, v)[0]


def inner(pieces):
    flat = shape(PIECES * PROWS, LANES)
    return call(inner_kernel, [VM], [(flat, VM)], [], 2 * 10**9, 10**6, "inner")(pieces.reshape(flat.shape))[0]


def spread(y, before, rows):
    return call(spread_kernel, [SM, VM, VM], [(shape(PIECES * PROWS, LANES), VM)], [], 10**6, 10**6, "spread")(
        y, before, rows.reshape(-1, LANES)
    )[0]


def intra(core, fq, fk, v, sib):
    return call(
        intra_kernel, [SM, VM, VM, VM, VM],
        [(shape(*QF, dtype=BF16), HB), (shape(*BY_QUADS), HB), (shape(*DENS), HB)],
        [TURNED, TURNED, pltpu.VMEM(QF, BF16), WIDE, pltpu.VMEM(DENS, F32), pltpu.SemaphoreType.DMA((4, 4))],
        2 * 10**9, 16 * 10**6, "intra",
    )(core, fq, fk, v, sib)


def window(start, q, k, v, hk, hv):
    return call(
        window_kernel, [SM] + [VM] * 5, [(shape(*BY_QUADS), HB)], [WIDE, pltpu.SemaphoreType.DMA((4,))],
        2 * 10**9, 16 * 10**6, "window",
    )(start, q, k, v, hk, hv)[0]


OUT = (shape(ROWS, VALUES, dtype=BF16), HB)
OUT_SCRATCH = [pltpu.VMEM(HALF, BF16), pltpu.SemaphoreType.DMA((2,))]


def stage(core, qf, num, den, win):
    half = [(shape(*HALF_QF, dtype=BF16), VM), (shape(*HALF), VM)]
    return call(
        stage_kernel, [SM] + [HB] * 4, half + [(shape(*HALF), VM)] + half + [(shape(*DENS), VM)],
        [pltpu.SemaphoreType.DMA((8,))], 10**9, 10**7, "stage",
    )(core, qf, num, den, win)


def final_first(core, prior, qf, num, den, own_win, win):
    return call(
        first_kernel, [SM] + [VM] * 5 + [HB], [(shape(*HALF, dtype=BF16), VM), (shape(*HALF), VM)],
        [pltpu.SemaphoreType.DMA((1,))], 2 * 10**9, 10**6, "first",
    )(core, prior, qf, num, den, own_win, win)


def final_second(core, prior, qf, num, den, win, done):
    return call(
        second_kernel, [SM] + [VM] * 6, [(shape(ROWS, VALUES, dtype=BF16), HB)],
        [pltpu.VMEM(HALF, BF16), pltpu.SemaphoreType.DMA((2, 2))], 2 * 10**9, 10**6, "second",
    )(core, prior, qf, num, den, win, done)[0]


def exchange(array, axes):
    return lax.all_to_all(array, axes, split_axis=0, concat_axis=0, tiled=True)


def swap(array):
    return lax.ppermute(array, "c", [(0, 1), (1, 0)])


def scalar(value):
    return jnp.asarray(value, jnp.int32).reshape(1)


def after(first, *arrays):
    return lax.optimization_barrier((first, *arrays))


def body(fq, fk, v, wq, wk):
    core = scalar(lax.axis_index("c"))
    start = scalar(lax.axis_index(AXES))
    state = own_state(core, fk, v)
    sib = swap(state)
    half = PAIRS // 2
    chip = (state[:half] + sib[half:]).reshape(PIECES, *PIECE)
    chip, fq, fk = after(chip, fq, fk)
    pieces = exchange(chip, ("x", "z"))
    qf, num, den = intra(core, fq, fk, v, sib)
    count = lax.axis_size(AXES)
    pairs = [(i, i + 1) for i in range(count - 1)]
    qf, wk_out, v_out = after(qf, wk, v)
    hk = lax.ppermute(wk_out, AXES, pairs)
    hv = lax.ppermute(v_out, AXES, pairs)
    pieces, qf, num, den = after(pieces, qf, num, den)
    total = jnp.broadcast_to(jnp.sum(pieces, 0), (8, *PIECE))
    total, pieces = after(total, pieces)
    rows = exchange(total, "y")
    before = inner(pieces)
    rows, before = after(rows, before)
    back = spread(scalar(lax.axis_index("y")), before, rows)
    back, wq = after(back.reshape(PIECES, *PIECE), wq)
    mine = exchange(back, ("x", "z"))
    win = window(start, wq, wk, v, hk, hv)
    staged = stage(core, qf, num, den, win)
    mine, *staged = after(mine, *staged)
    qf0, num0, win0, qf1, num1, den = staged
    mine = mine.reshape(half, PAIR_ROWS, LANES)
    other = swap(mine)
    done, win1 = final_first(core, mine, qf0, num0, den, win0, win)
    return final_second(core, other, qf1, num1, den, win1, done)


def solution(mesh):
    finer = Mesh(mesh.devices.reshape(8, 4, 8, 2), AXES)
    placed = P(AXES, None)
    return jax.shard_map(
        body, mesh=finer, in_specs=(placed,) * 5, out_specs=placed, check_vma=False
    )
```

```python
import functools

import jax
import jax.numpy as jnp
import numpy as np
from jax import lax
from jax.experimental import pallas as pl
from jax.experimental.pallas import tpu as pltpu
from jax.sharding import Mesh
from jax.sharding import PartitionSpec as P

HEADS = 16
PAIRS = HEADS // 2
DIM = 16
ROWS = 256
QUADS = 4
FEATS = 153
FROWS = 160
PIECES = 32
PAIR_ROWS = 160
PROWS = 20
PIECE = (PROWS // 4, 4, 128)
TAIL = slice(152, 160)
VALUES = HEADS * 64
LANES = 128
AXES = ("y", "x", "z", "c")
F32 = jnp.float32
BF16 = jnp.bfloat16
W_DIAG = np.float32(1.0 / np.sqrt(2.0 * DIM))
W_OFF = np.float32(1.0 / np.sqrt(1.0 * DIM))
SCALE = np.float32(1.0 / DIM**0.25)
NT = (((1,), (1,)), ((), ()))


def features(x):
    twice = jnp.concatenate([x, x], 0)
    quarter = twice * W_OFF
    parts = [x * SCALE, x * x * W_DIAG]
    for shift in range(1, 8):
        parts.append(x * quarter[shift : shift + DIM])
    parts.append(x[:8] * quarter[8:16])
    one = lax.broadcasted_iota(jnp.int32, (8, x.shape[1]), 0) == 0
    parts.append(jnp.where(one, F32(1.0), F32(0.0)))
    return jnp.concatenate(parts, 0)


def low_lanes(rows):
    return lax.broadcasted_iota(jnp.int32, (rows, LANES), 1) < 64


def half_state(first, kt_ref, v_ref):
    lane = lax.broadcasted_iota(jnp.int32, (FROWS, LANES), 1)
    low = lane < 64
    vlow = low_lanes(ROWS)
    zcols = jnp.zeros((FROWS, LANES), F32)
    states = []
    for i in range(PAIRS // 2):
        pair = first + i
        x = kt_ref[pl.ds(pl.multiple_of(pair * 32, 32), 32), :]
        v = v_ref[:, pl.ds(pl.multiple_of(pair * LANES, LANES), LANES)]
        one = jnp.ones_like(v)
        fa = features(x[:DIM]).astype(BF16)
        fb = features(x[DIM:]).astype(BF16)
        sa = jnp.dot(fa, jnp.where(vlow, v, one), preferred_element_type=F32)
        sb = jnp.dot(fb, jnp.where(vlow, one, v), preferred_element_type=F32)
        states.append(jnp.where(low, sa, sb))
        z = jnp.where(low, sb, sa)
        zcols = jnp.where((lane == i) | (lane == 64 + i), z, zcols)
    zrows = zcols.T
    blank = jnp.zeros((8, 2 * LANES - FROWS), F32)
    row = lax.broadcasted_iota(jnp.int32, (8, LANES), 0)
    for i in range(PAIRS // 2):
        tail = states[i][TAIL]
        for at, src in ((1, 64 + i), (3, i)):
            z = jnp.concatenate([jnp.broadcast_to(zrows[src : src + 1], (8, FROWS)), blank], 1)
            tail = jnp.where(row == at, z[:, :LANES], tail)
            tail = jnp.where(row == at + 1, z[:, LANES:], tail)
        states[i] = jnp.concatenate([states[i][: TAIL.start], tail], 0)
    return states


def other_kernel(core_ref, fk_hbm, v_hbm, out_ref, kt_ref, v_ref, fk_ref, sems):
    copies = [
        pltpu.make_async_copy(fk_hbm, fk_ref, sems.at[0]),
        pltpu.make_async_copy(v_hbm, v_ref, sems.at[1]),
    ]
    for copy in copies:
        copy.start()
    copies[0].wait()
    kt_ref[...] = fk_ref[...].astype(F32).T
    copies[1].wait()
    for i, state in enumerate(half_state((1 - core_ref[0]) * (PAIRS // 2), kt_ref, v_ref)):
        out_ref[i] = state


def chip_kernel(core_ref, kt_ref, v_ref, got_ref, mine_ref, chip_ref):
    for i, state in enumerate(half_state(core_ref[0] * (PAIRS // 2), kt_ref, v_ref)):
        mine_ref[i] = state
        chip_ref[i] = state + got_ref[i]


def inner_kernel(p_ref, out_ref):
    run = jnp.zeros((PROWS, LANES), F32)
    for k in range(PIECES):
        at = slice(PROWS * k, PROWS * (k + 1))
        out_ref[at] = run
        run = run + p_ref[at]


def spread_kernel(y_ref, inner_ref, py_ref, out_ref):
    y = y_ref[0]
    outer = jnp.zeros((PROWS, LANES), F32)
    for k in range(8):
        outer = outer + jnp.where(k < y, py_ref[PROWS * k : PROWS * (k + 1)], F32(0.0))
    twice = jnp.concatenate([outer, outer], 0)
    for k in range(PIECES // 2):
        at = slice(2 * PROWS * k, 2 * PROWS * (k + 1))
        out_ref[at] = inner_ref[at] + twice


def split3(x):
    hi = x.astype(BF16)
    rest = x - hi.astype(F32)
    mid = rest.astype(BF16)
    lo = (rest - mid.astype(F32)).astype(BF16)
    return hi, mid, lo


def norm_columns(tails):
    rows = []
    for tail in tails:
        for row in (1, 3):
            rows.append(jnp.concatenate([tail[row : row + 1], tail[row + 1 : row + 2]], 1))
    rows.append(jnp.zeros((LANES - len(rows), 2 * LANES), F32))
    return jnp.concatenate(rows, 0).T[:FROWS]


def laid_out(w, slot):
    gap = jnp.zeros((32, w.shape[1]), w.dtype)
    return jnp.concatenate([w[:LANES]] + [gap] * slot + [w[LANES:]] + [gap] * (3 - slot), 0)


def cross(qfs, s, zcols, at, slot):
    low, tlow = low_lanes(FROWS), low_lanes(ROWS)
    s = jnp.where(lax.broadcasted_iota(jnp.int32, s.shape, 0) < FEATS, s, F32(0.0))
    res = []
    for h in range(2):
        z = jnp.broadcast_to(zcols[:, at + h : at + h + 1], (FROWS, LANES))
        parts = split3(jnp.where(low, s, z) if h == 0 else jnp.where(low, z, s))
        hi, mid, lo = (laid_out(part, slot + h) for part in parts)
        big = jnp.dot(qfs[h], jnp.concatenate([hi, mid], 1), preferred_element_type=F32)
        res.append(big[:, :LANES] + (big[:, LANES:] + jnp.dot(qfs[h], lo, preferred_element_type=F32)))
    return jnp.where(tlow, res[0], res[1]), jnp.where(tlow, res[1], res[0])


def intra_kernel(core_ref, fq_ref, fk_ref, v_ref, low_ref, high_ref, qf_hbm, num_hbm, den_hbm, qt_ref, kt_ref, qf_ref, num_ref, den_ref, sems):
    second = core_ref[0] == 1
    qt_ref[...] = fq_ref[...].astype(F32).T
    kt_ref[...] = fk_ref[...].astype(F32).T
    low = low_lanes(ROWS)
    lane = lax.broadcasted_iota(jnp.int32, (ROWS, LANES), 1)
    causal = lax.broadcasted_iota(jnp.int32, (ROWS, ROWS), 0) >= lax.broadcasted_iota(
        jnp.int32, (ROWS, ROWS), 1
    )
    sibs = [(low_ref, high_ref)[i // 4].at[i % 4] for i in range(PAIRS)]
    zcols = norm_columns([sib[TAIL] for sib in sibs])
    zcols = jnp.where(second, zcols, F32(0.0))
    all_dens = jnp.zeros((ROWS, LANES), F32)
    copies = []

    def send(src, dst, k, quad):
        copy = pltpu.make_async_copy(src, dst, sems.at[k, quad])
        copy.start()
        copies.append(copy)

    for quad in range(QUADS):
        dens, rounded, mains, rests = [], [], [], []
        for h in range(4 * quad, 4 * quad + 4):
            f = features(qt_ref[h * DIM : (h + 1) * DIM, :])
            main = f[:LANES].T.astype(BF16)
            qf_ref[h] = main
            mains.append(main)
            rests.append(f[LANES:])
        rest = jnp.concatenate(rests, 0).T.astype(BF16)
        qf_ref[HEADS + quad] = rest
        qfs = [jnp.concatenate([main, rest], 1) for main in mains]
        for slot in range(4):
            h = 4 * quad + slot
            kf = laid_out(features(kt_ref[h * DIM : (h + 1) * DIM, :]).astype(BF16), slot)
            a = jnp.dot(qfs[slot], kf, preferred_element_type=F32)
            a = jnp.where(causal, a, F32(0.0))
            dens.append(jnp.sum(a, -1, keepdims=True))
            rounded.append(a.astype(BF16))
        wide = slice(quad * 256, (quad + 1) * 256)
        nums = jnp.dot(jnp.concatenate(rounded, 0), v_ref[:, wide], preferred_element_type=F32)
        for p in range(2):
            pair = 2 * quad + p
            s = jnp.where(second, sibs[pair][...], F32(0.0))
            num, den = cross(qfs[2 * p : 2 * p + 2], s, zcols, 2 * pair, 2 * p)
            here = slice(p * LANES, (p + 1) * LANES)
            n0 = nums[2 * p * ROWS : (2 * p + 1) * ROWS, here]
            n1 = nums[(2 * p + 1) * ROWS : (2 * p + 2) * ROWS, here]
            num_ref[quad, :, here] = num + jnp.where(low, n0, n1)
            den = den + jnp.where(low, dens[2 * p + 1], dens[2 * p])
            place = jnp.where(second, (pair + PAIRS // 2) % PAIRS, pair)
            all_dens = jnp.where(lane % 64 == place, den, all_dens)
        heads = pl.ds(4 * quad, 4)
        send(qf_ref.at[heads], qf_hbm.at[heads], 0, quad)
        send(qf_ref.at[pl.ds(HEADS + quad, 1)], qf_hbm.at[pl.ds(HEADS + quad, 1)], 1, quad)
        send(num_ref.at[quad], num_hbm.at[quad], 2, quad)
    den_ref[...] = all_dens
    send(den_ref, den_hbm, 3, 0)
    for copy in copies:
        copy.wait()


def window_kernel(start_ref, q_ref, k_ref, v_ref, hk_ref, hv_ref, out_hbm, out_ref, sems):
    half = ROWS // 2
    inside = start_ref[0] > 0
    r = lax.broadcasted_iota(jnp.int32, (4 * half, ROWS), 0) % half
    c = lax.broadcasted_iota(jnp.int32, (4 * half, ROWS), 1)
    masks = (
        ((c > r) & inside, (c <= r)[:, :half]),
        ((c > r)[:, :half] & inside, c <= r + half),
    )
    worst = F32(-1e30)
    head = lax.broadcasted_iota(jnp.int32, (half, 256), 1) // 64
    copies = []
    for quad in range(PAIRS // 2):
        lanes = slice(quad * 256, (quad + 1) * 256)
        for b in range(2):
            mine = slice(half * b, half * (b + 1))
            q = q_ref[mine, lanes] * BF16(0.125)
            hs = slice(half * b, ROWS)
            os = slice(0, half * (b + 1))
            qs = jnp.concatenate([jnp.where(head == h, q, jnp.zeros_like(q)) for h in range(4)], 0)
            lh = lax.dot_general(qs, hk_ref[hs, lanes], NT, preferred_element_type=F32)
            lo = lax.dot_general(qs, k_ref[os, lanes], NT, preferred_element_type=F32)
            lh = jnp.where(masks[b][0], lh, worst)
            lo = jnp.where(masks[b][1], lo, worst)
            peak = jnp.maximum(jnp.max(lh, -1, keepdims=True), jnp.max(lo, -1, keepdims=True))
            eh = jnp.exp(lh - peak)
            eo = jnp.exp(lo - peak)
            inv = F32(1.0) / (jnp.sum(eh, -1, keepdims=True) + jnp.sum(eo, -1, keepdims=True))
            ph = (eh * inv).astype(BF16)
            po = (eo * inv).astype(BF16)
            o = jnp.dot(ph, hv_ref[hs, lanes], preferred_element_type=F32) + jnp.dot(
                po, v_ref[os, lanes], preferred_element_type=F32
            )
            res = o[:half]
            for h in range(1, 4):
                res = jnp.where(head == h, o[h * half : (h + 1) * half], res)
            out_ref[quad, mine] = res
        copy = pltpu.make_async_copy(out_ref.at[quad], out_hbm.at[quad], sems.at[quad])
        copy.start()
        copies.append(copy)
    for copy in copies:
        copy.wait()


def finish(part, p_ref, qf_ref, num_ref, den_ref, win_ref, out_ref, q, zcols):
    low = low_lanes(ROWS)
    rest = qf_ref[8 + q]
    for p in range(2):
        i = 2 * q + p
        qfs = [jnp.concatenate([qf_ref[2 * i + h], rest], 1) for h in range(2)]
        num, den = cross(qfs, p_ref[i], zcols, 2 * i, 2 * p)
        at = PAIRS // 2 * part + i
        den = den + jnp.where(low, den_ref[:, at : at + 1], den_ref[:, 64 + at : 65 + at])
        here = slice(p * LANES, (p + 1) * LANES)
        linear = (num + num_ref[q, :, here]) / pltpu.roll(den, 64, 1)
        out_ref[q, :, here] = (linear + win_ref[q, :, here]).astype(BF16)


def norms_of(p_ref):
    return norm_columns([p_ref[i, TAIL] for i in range(PAIRS // 2)])


def leave(out_ref, out_hbm, half, q, sems):
    lanes = pl.ds(pl.multiple_of(half * 512 + q * 256, 256), 256)
    copy = pltpu.make_async_copy(out_ref.at[q], out_hbm.at[:, lanes], sems.at[q])
    copy.start()
    return copy


def stage_kernel(core_ref, qf_hbm, num_hbm, den_hbm, win_hbm, *refs):
    core = core_ref[0]
    qf_ref, num_ref, win_ref, qf2_ref, num2_ref, den_ref, sems = refs
    copies = []
    for k, (src, dst) in enumerate(
        (
            (den_hbm, den_ref),
            (qf_hbm.at[pl.ds(8 * core, 8)], qf_ref.at[pl.ds(0, 8)]),
            (qf_hbm.at[pl.ds(HEADS + 2 * core, 2)], qf_ref.at[pl.ds(8, 2)]),
            (num_hbm.at[pl.ds(2 * core, 2)], num_ref),
            (qf_hbm.at[pl.ds(8 - 8 * core, 8)], qf2_ref.at[pl.ds(0, 8)]),
            (qf_hbm.at[pl.ds(HEADS + 2 - 2 * core, 2)], qf2_ref.at[pl.ds(8, 2)]),
            (num_hbm.at[pl.ds(2 - 2 * core, 2)], num2_ref),
            (win_hbm.at[pl.ds(2 * core, 2)], win_ref),
        )
    ):
        copies.append(pltpu.make_async_copy(src, dst, sems.at[k]))
    for copy in copies:
        copy.start()
    for copy in copies:
        copy.wait()


def first_kernel(core_ref, p_ref, qf_ref, num_ref, den_ref, win_ref, win_hbm, out_ref, win2_ref, sem):
    win = pltpu.make_async_copy(win_hbm.at[pl.ds(2 - 2 * core_ref[0], 2)], win2_ref, sem.at[0])
    win.start()
    zcols = norms_of(p_ref)
    for q in range(2):
        finish(0, p_ref, qf_ref, num_ref, den_ref, win_ref, out_ref, q, zcols)
    win.wait()


def second_kernel(core_ref, p_ref, qf_ref, num_ref, den_ref, win_ref, done_ref, out_hbm, out_ref, sems):
    core = core_ref[0]
    leaving = [leave(done_ref, out_hbm, core, q, sems.at[0]) for q in range(2)]
    zcols = norms_of(p_ref)
    for q in range(2):
        finish(1, p_ref, qf_ref, num_ref, den_ref, win_ref, out_ref, q, zcols)
        leaving.append(leave(out_ref, out_hbm, 1 - core, q, sems.at[1]))
    for copy in leaving:
        copy.wait()


def spec(kind=pltpu.VMEM):
    return pl.BlockSpec(memory_space=kind)


def call(kernel, ins, outs, scratch, flops, moved, name):
    made = pl.pallas_call(
        kernel,
        out_shape=[pltpu.HBM(o.shape, o.dtype) if k == HB else o for o, k in outs],
        in_specs=[spec(k) for k in ins],
        out_specs=[spec(k) for _, k in outs],
        scratch_shapes=scratch,
        compiler_params=pltpu.CompilerParams(vmem_limit_bytes=40 * 2**20),
        cost_estimate=pl.CostEstimate(flops=flops, bytes_accessed=moved, transcendentals=0),
        name=name,
    )
    return lambda *arrays: made(
        *(pltpu.with_memory_space_constraint(a, k) if k == HB else a for a, k in zip(arrays, ins, strict=True))
    )


def shape(*dims, dtype=F32):
    return jax.ShapeDtypeStruct(dims, dtype)


SM, VM, HB = pltpu.SMEM, pltpu.VMEM, pltpu.HBM
TURNED = pltpu.VMEM((256, ROWS), F32)
WIDE = pltpu.VMEM((QUADS, ROWS, 256), F32)
QF = (HEADS + QUADS, ROWS, LANES)
DENS = (ROWS, LANES)
BY_QUADS = (QUADS, ROWS, 256)
HALF_QF = (10, ROWS, LANES)
HALF = (2, ROWS, 256)


STATES = (PAIRS // 2, PAIR_ROWS, LANES)


def other_state(core, fk, v):
    return call(
        other_kernel, [SM, HB, HB],
        [(shape(*STATES), VM), (shape(256, ROWS), VM), (shape(ROWS, VALUES, dtype=BF16), VM)],
        [pltpu.VMEM((ROWS, 256), BF16), pltpu.SemaphoreType.DMA((2,))], 10**9, 5 * 10**6, "other",
    )(core, fk, v)


def chip_state(core, kt, v, got):
    return call(
        chip_kernel, [SM, VM, VM, VM], [(shape(*STATES), VM), (shape(*STATES), VM)], [], 10**9, 10**6, "chip"
    )(core, kt, v, got)


def inner(pieces):
    flat = shape(PIECES * PROWS, LANES)
    return call(inner_kernel, [VM], [(flat, VM)], [], 2 * 10**9, 10**6, "inner")(pieces.reshape(flat.shape))[0]


def spread(y, before, rows):
    return call(spread_kernel, [SM, VM, VM], [(shape(PIECES * PROWS, LANES), VM)], [], 10**6, 10**6, "spread")(
        y, before, rows.reshape(-1, LANES)
    )[0]


def intra(core, fq, fk, v, low, high):
    return call(
        intra_kernel, [SM] + [VM] * 5,
        [(shape(*QF, dtype=BF16), HB), (shape(*BY_QUADS), HB), (shape(*DENS), HB)],
        [TURNED, TURNED, pltpu.VMEM(QF, BF16), WIDE, pltpu.VMEM(DENS, F32), pltpu.SemaphoreType.DMA((4, 4))],
        2 * 10**9, 16 * 10**6, "intra",
    )(core, fq, fk, v, low, high)


def window(start, q, k, v, hk, hv):
    return call(
        window_kernel, [SM] + [VM] * 5, [(shape(*BY_QUADS), HB)], [WIDE, pltpu.SemaphoreType.DMA((4,))],
        2 * 10**9, 16 * 10**6, "window",
    )(start, q, k, v, hk, hv)[0]


OUT = (shape(ROWS, VALUES, dtype=BF16), HB)
OUT_SCRATCH = [pltpu.VMEM(HALF, BF16), pltpu.SemaphoreType.DMA((2,))]


def stage(core, qf, num, den, win):
    half = [(shape(*HALF_QF, dtype=BF16), VM), (shape(*HALF), VM)]
    return call(
        stage_kernel, [SM] + [HB] * 4, half + [(shape(*HALF), VM)] + half + [(shape(*DENS), VM)],
        [pltpu.SemaphoreType.DMA((8,))], 10**9, 10**7, "stage",
    )(core, qf, num, den, win)


def final_first(core, prior, qf, num, den, own_win, win):
    return call(
        first_kernel, [SM] + [VM] * 5 + [HB], [(shape(*HALF, dtype=BF16), VM), (shape(*HALF), VM)],
        [pltpu.SemaphoreType.DMA((1,))], 2 * 10**9, 10**6, "first",
    )(core, prior, qf, num, den, own_win, win)


def final_second(core, prior, qf, num, den, win, done):
    return call(
        second_kernel, [SM] + [VM] * 6, [(shape(ROWS, VALUES, dtype=BF16), HB)],
        [pltpu.VMEM(HALF, BF16), pltpu.SemaphoreType.DMA((2, 2))], 2 * 10**9, 10**6, "second",
    )(core, prior, qf, num, den, win, done)[0]


def exchange(array, axes):
    return lax.all_to_all(array, axes, split_axis=0, concat_axis=0, tiled=True)


def swap(array):
    return lax.ppermute(array, "c", [(0, 1), (1, 0)])


def scalar(value):
    return jnp.asarray(value, jnp.int32).reshape(1)


def after(first, *arrays):
    return lax.optimization_barrier((first, *arrays))


def body(fq, fk, v, wq, wk):
    core = scalar(lax.axis_index("c"))
    start = scalar(lax.axis_index(AXES))
    half = PAIRS // 2
    state, turned, held = other_state(core, fk, v)
    got = swap(state)
    own, chip = chip_state(core, turned, held, got)
    chip, own = after(chip.reshape(PIECES, *PIECE), own)
    pieces = exchange(chip, ("x", "z"))
    low, wk_out, v_out = after(swap(own), wk, v)
    count = lax.axis_size(AXES)
    pairs = [(i, i + 1) for i in range(count - 1)]
    hk = lax.ppermute(wk_out, AXES, pairs)
    hv = lax.ppermute(v_out, AXES, pairs)
    pieces, low = after(pieces, low)
    total = jnp.broadcast_to(jnp.sum(pieces, 0), (8, *PIECE))
    total, pieces, low, fq, fk = after(total, pieces, low, fq, fk)
    rows = exchange(total, "y")
    before = inner(pieces)
    qf, num, den = intra(core, fq, fk, v, low, got)
    rows, before, qf, num, den = after(rows, before, qf, num, den)
    back = spread(scalar(lax.axis_index("y")), before, rows)
    back, wq = after(back.reshape(PIECES, *PIECE), wq)
    mine = exchange(back, ("x", "z"))
    win = window(start, wq, wk, v, hk, hv)
    staged = stage(core, qf, num, den, win)
    mine, *staged = after(mine, *staged)
    qf0, num0, win0, qf1, num1, den = staged
    mine = mine.reshape(half, PAIR_ROWS, LANES)
    other = swap(mine)
    done, win1 = final_first(core, mine, qf0, num0, den, win0, win)
    return final_second(core, other, qf1, num1, den, win1, done)


def solution(mesh):
    finer = Mesh(mesh.devices.reshape(8, 4, 8, 2), AXES)
    placed = P(AXES, None)
    return jax.shard_map(
        body, mesh=finer, in_specs=(placed,) * 5, out_specs=placed, check_vma=False
    )
```

```python
import functools

import jax
import jax.numpy as jnp
import numpy as np
from jax import lax
from jax.experimental import pallas as pl
from jax.experimental.pallas import tpu as pltpu
from jax.sharding import Mesh
from jax.sharding import PartitionSpec as P

HEADS = 16
PAIRS = HEADS // 2
DIM = 16
ROWS = 256
QUADS = 4
FEATS = 153
FROWS = 160
PIECES = 32
PAIR_ROWS = 160
PROWS = 20
PIECE = (PROWS // 4, 4, 128)
TAIL = slice(152, 160)
VALUES = HEADS * 64
LANES = 128
AXES = ("y", "x", "z", "c")
F32 = jnp.float32
BF16 = jnp.bfloat16
W_DIAG = np.float32(1.0 / np.sqrt(2.0 * DIM))
W_OFF = np.float32(1.0 / np.sqrt(1.0 * DIM))
SCALE = np.float32(1.0 / DIM**0.25)
NT = (((1,), (1,)), ((), ()))


def features(x):
    twice = jnp.concatenate([x, x], 0)
    quarter = twice * W_OFF
    parts = [x * SCALE, x * x * W_DIAG]
    for shift in range(1, 8):
        parts.append(x * quarter[shift : shift + DIM])
    parts.append(x[:8] * quarter[8:16])
    one = lax.broadcasted_iota(jnp.int32, (8, x.shape[1]), 0) == 0
    parts.append(jnp.where(one, F32(1.0), F32(0.0)))
    return jnp.concatenate(parts, 0)


def low_lanes(rows):
    return lax.broadcasted_iota(jnp.int32, (rows, LANES), 1) < 64


def half_state(first, kt_ref, v_ref):
    lane = lax.broadcasted_iota(jnp.int32, (FROWS, LANES), 1)
    low = lane < 64
    vlow = low_lanes(ROWS)
    zcols = jnp.zeros((FROWS, LANES), F32)
    states = []
    for i in range(PAIRS // 2):
        pair = first + i
        x = kt_ref[pl.ds(pl.multiple_of(pair * 32, 32), 32), :]
        v = v_ref[:, pl.ds(pl.multiple_of(pair * LANES, LANES), LANES)]
        one = jnp.ones_like(v)
        fa = features(x[:DIM]).astype(BF16)
        fb = features(x[DIM:]).astype(BF16)
        sa = jnp.dot(fa, jnp.where(vlow, v, one), preferred_element_type=F32)
        sb = jnp.dot(fb, jnp.where(vlow, one, v), preferred_element_type=F32)
        states.append(jnp.where(low, sa, sb))
        z = jnp.where(low, sb, sa)
        zcols = jnp.where((lane == i) | (lane == 64 + i), z, zcols)
    zrows = zcols.T
    blank = jnp.zeros((8, 2 * LANES - FROWS), F32)
    row = lax.broadcasted_iota(jnp.int32, (8, LANES), 0)
    for i in range(PAIRS // 2):
        tail = states[i][TAIL]
        for at, src in ((1, 64 + i), (3, i)):
            z = jnp.concatenate([jnp.broadcast_to(zrows[src : src + 1], (8, FROWS)), blank], 1)
            tail = jnp.where(row == at, z[:, :LANES], tail)
            tail = jnp.where(row == at + 1, z[:, LANES:], tail)
        states[i] = jnp.concatenate([states[i][: TAIL.start], tail], 0)
    return states


def other_kernel(core_ref, fk_hbm, v_hbm, out_ref, kt_ref, v_ref, fk_ref, sems):
    copies = [
        pltpu.make_async_copy(fk_hbm, fk_ref, sems.at[0]),
        pltpu.make_async_copy(v_hbm, v_ref, sems.at[1]),
    ]
    for copy in copies:
        copy.start()
    copies[0].wait()
    kt_ref[...] = fk_ref[...].astype(F32).T
    copies[1].wait()
    for i, state in enumerate(half_state((1 - core_ref[0]) * (PAIRS // 2), kt_ref, v_ref)):
        out_ref[i] = state


def chip_kernel(core_ref, kt_ref, v_ref, got_ref, mine_ref, chip_ref):
    for i, state in enumerate(half_state(core_ref[0] * (PAIRS // 2), kt_ref, v_ref)):
        mine_ref[i] = state
        chip_ref[i] = state + got_ref[i]


def spread_kernel(y_ref, p_ref, py_ref, out_ref):
    y = y_ref[0]
    run = jnp.zeros((PROWS, LANES), F32)
    for k in range(8):
        run = run + jnp.where(k < y, py_ref[PROWS * k : PROWS * (k + 1)], F32(0.0))
    for k in range(PIECES):
        at = slice(PROWS * k, PROWS * (k + 1))
        out_ref[at] = run
        run = run + p_ref[at]


def split3(x):
    hi = x.astype(BF16)
    rest = x - hi.astype(F32)
    mid = rest.astype(BF16)
    lo = (rest - mid.astype(F32)).astype(BF16)
    return hi, mid, lo


def norm_columns(tails):
    rows = []
    for tail in tails:
        for row in (1, 3):
            rows.append(jnp.concatenate([tail[row : row + 1], tail[row + 1 : row + 2]], 1))
    rows.append(jnp.zeros((LANES - len(rows), 2 * LANES), F32))
    return jnp.concatenate(rows, 0).T[:FROWS]


def laid_out(w, slot):
    gap = jnp.zeros((32, w.shape[1]), w.dtype)
    return jnp.concatenate([w[:LANES]] + [gap] * slot + [w[LANES:]] + [gap] * (3 - slot), 0)


def cross(qfs, s, zcols, at, slot):
    low, tlow = low_lanes(FROWS), low_lanes(ROWS)
    s = jnp.where(lax.broadcasted_iota(jnp.int32, s.shape, 0) < FEATS, s, F32(0.0))
    res = []
    for h in range(2):
        z = jnp.broadcast_to(zcols[:, at + h : at + h + 1], (FROWS, LANES))
        parts = split3(jnp.where(low, s, z) if h == 0 else jnp.where(low, z, s))
        hi, mid, lo = (laid_out(part, slot + h) for part in parts)
        big = jnp.dot(qfs[h], jnp.concatenate([hi, mid], 1), preferred_element_type=F32)
        res.append(big[:, :LANES] + (big[:, LANES:] + jnp.dot(qfs[h], lo, preferred_element_type=F32)))
    return jnp.where(tlow, res[0], res[1]), jnp.where(tlow, res[1], res[0])


def intra_kernel(core_ref, fq_ref, fk_ref, v_ref, low_ref, high_ref, qf_hbm, num_hbm, den_hbm, qt_ref, kt_ref, qf_ref, num_ref, den_ref, sems):
    second = core_ref[0] == 1
    qt_ref[...] = fq_ref[...].astype(F32).T
    kt_ref[...] = fk_ref[...].astype(F32).T
    low = low_lanes(ROWS)
    lane = lax.broadcasted_iota(jnp.int32, (ROWS, LANES), 1)
    causal = lax.broadcasted_iota(jnp.int32, (ROWS, ROWS), 0) >= lax.broadcasted_iota(
        jnp.int32, (ROWS, ROWS), 1
    )
    sibs = [(low_ref, high_ref)[i // 4].at[i % 4] for i in range(PAIRS)]
    zcols = norm_columns([sib[TAIL] for sib in sibs])
    zcols = jnp.where(second, zcols, F32(0.0))
    all_dens = jnp.zeros((ROWS, LANES), F32)
    copies = []

    def send(src, dst, k, quad):
        copy = pltpu.make_async_copy(src, dst, sems.at[k, quad])
        copy.start()
        copies.append(copy)

    for quad in range(QUADS):
        dens, rounded, mains, rests = [], [], [], []
        for h in range(4 * quad, 4 * quad + 4):
            f = features(qt_ref[h * DIM : (h + 1) * DIM, :])
            main = f[:LANES].T.astype(BF16)
            qf_ref[h] = main
            mains.append(main)
            rests.append(f[LANES:])
        rest = jnp.concatenate(rests, 0).T.astype(BF16)
        qf_ref[HEADS + quad] = rest
        qfs = [jnp.concatenate([main, rest], 1) for main in mains]
        for slot in range(4):
            h = 4 * quad + slot
            kf = laid_out(features(kt_ref[h * DIM : (h + 1) * DIM, :]).astype(BF16), slot)
            a = jnp.dot(qfs[slot], kf, preferred_element_type=F32)
            a = jnp.where(causal, a, F32(0.0))
            dens.append(jnp.sum(a, -1, keepdims=True))
            rounded.append(a.astype(BF16))
        wide = slice(quad * 256, (quad + 1) * 256)
        nums = jnp.dot(jnp.concatenate(rounded, 0), v_ref[:, wide], preferred_element_type=F32)
        for p in range(2):
            pair = 2 * quad + p
            s = jnp.where(second, sibs[pair][...], F32(0.0))
            num, den = cross(qfs[2 * p : 2 * p + 2], s, zcols, 2 * pair, 2 * p)
            here = slice(p * LANES, (p + 1) * LANES)
            n0 = nums[2 * p * ROWS : (2 * p + 1) * ROWS, here]
            n1 = nums[(2 * p + 1) * ROWS : (2 * p + 2) * ROWS, here]
            num_ref[quad, :, here] = num + jnp.where(low, n0, n1)
            den = den + jnp.where(low, dens[2 * p + 1], dens[2 * p])
            place = jnp.where(second, (pair + PAIRS // 2) % PAIRS, pair)
            all_dens = jnp.where(lane % 64 == place, den, all_dens)
        heads = pl.ds(4 * quad, 4)
        send(qf_ref.at[heads], qf_hbm.at[heads], 0, quad)
        send(qf_ref.at[pl.ds(HEADS + quad, 1)], qf_hbm.at[pl.ds(HEADS + quad, 1)], 1, quad)
        send(num_ref.at[quad], num_hbm.at[quad], 2, quad)
    den_ref[...] = all_dens
    send(den_ref, den_hbm, 3, 0)
    for copy in copies:
        copy.wait()


def window_kernel(start_ref, q_ref, k_ref, v_ref, hk_ref, hv_ref, out_hbm, out_ref, sems):
    half = ROWS // 2
    inside = start_ref[0] > 0
    r = lax.broadcasted_iota(jnp.int32, (4 * half, ROWS), 0) % half
    c = lax.broadcasted_iota(jnp.int32, (4 * half, ROWS), 1)
    masks = (
        ((c > r) & inside, (c <= r)[:, :half]),
        ((c > r)[:, :half] & inside, c <= r + half),
    )
    worst = F32(-1e30)
    head = lax.broadcasted_iota(jnp.int32, (half, 256), 1) // 64
    copies = []
    for quad in range(PAIRS // 2):
        lanes = slice(quad * 256, (quad + 1) * 256)
        for b in range(2):
            mine = slice(half * b, half * (b + 1))
            q = q_ref[mine, lanes] * BF16(0.125)
            hs = slice(half * b, ROWS)
            os = slice(0, half * (b + 1))
            qs = jnp.concatenate([jnp.where(head == h, q, jnp.zeros_like(q)) for h in range(4)], 0)
            lh = lax.dot_general(qs, hk_ref[hs, lanes], NT, preferred_element_type=F32)
            lo = lax.dot_general(qs, k_ref[os, lanes], NT, preferred_element_type=F32)
            lh = jnp.where(masks[b][0], lh, worst)
            lo = jnp.where(masks[b][1], lo, worst)
            peak = jnp.maximum(jnp.max(lh, -1, keepdims=True), jnp.max(lo, -1, keepdims=True))
            eh = jnp.exp(lh - peak)
            eo = jnp.exp(lo - peak)
            inv = F32(1.0) / (jnp.sum(eh, -1, keepdims=True) + jnp.sum(eo, -1, keepdims=True))
            ph = (eh * inv).astype(BF16)
            po = (eo * inv).astype(BF16)
            o = jnp.dot(ph, hv_ref[hs, lanes], preferred_element_type=F32) + jnp.dot(
                po, v_ref[os, lanes], preferred_element_type=F32
            )
            res = o[:half]
            for h in range(1, 4):
                res = jnp.where(head == h, o[h * half : (h + 1) * half], res)
            out_ref[quad, mine] = res
        copy = pltpu.make_async_copy(out_ref.at[quad], out_hbm.at[quad], sems.at[quad])
        copy.start()
        copies.append(copy)
    for copy in copies:
        copy.wait()


def finish(part, p_ref, qf_ref, num_ref, den_ref, win_ref, out_ref, q, zcols):
    low = low_lanes(ROWS)
    rest = qf_ref[8 + q]
    for p in range(2):
        i = 2 * q + p
        qfs = [jnp.concatenate([qf_ref[2 * i + h], rest], 1) for h in range(2)]
        num, den = cross(qfs, p_ref[i], zcols, 2 * i, 2 * p)
        at = PAIRS // 2 * part + i
        den = den + jnp.where(low, den_ref[:, at : at + 1], den_ref[:, 64 + at : 65 + at])
        here = slice(p * LANES, (p + 1) * LANES)
        linear = (num + num_ref[q, :, here]) / pltpu.roll(den, 64, 1)
        out_ref[q, :, here] = (linear + win_ref[q, :, here]).astype(BF16)


def norms_of(p_ref):
    return norm_columns([p_ref[i, TAIL] for i in range(PAIRS // 2)])


def leave(out_ref, out_hbm, half, q, sems):
    lanes = pl.ds(pl.multiple_of(half * 512 + q * 256, 256), 256)
    copy = pltpu.make_async_copy(out_ref.at[q], out_hbm.at[:, lanes], sems.at[q])
    copy.start()
    return copy


def stage_kernel(core_ref, qf_hbm, num_hbm, den_hbm, win_hbm, *refs):
    core = core_ref[0]
    qf_ref, num_ref, win_ref, qf2_ref, num2_ref, den_ref, sems = refs
    copies = []
    for k, (src, dst) in enumerate(
        (
            (den_hbm, den_ref),
            (qf_hbm.at[pl.ds(8 * core, 8)], qf_ref.at[pl.ds(0, 8)]),
            (qf_hbm.at[pl.ds(HEADS + 2 * core, 2)], qf_ref.at[pl.ds(8, 2)]),
            (num_hbm.at[pl.ds(2 * core, 2)], num_ref),
            (qf_hbm.at[pl.ds(8 - 8 * core, 8)], qf2_ref.at[pl.ds(0, 8)]),
            (qf_hbm.at[pl.ds(HEADS + 2 - 2 * core, 2)], qf2_ref.at[pl.ds(8, 2)]),
            (num_hbm.at[pl.ds(2 - 2 * core, 2)], num2_ref),
            (win_hbm.at[pl.ds(2 * core, 2)], win_ref),
        )
    ):
        copies.append(pltpu.make_async_copy(src, dst, sems.at[k]))
    for copy in copies:
        copy.start()
    for copy in copies:
        copy.wait()


def first_kernel(core_ref, p_ref, qf_ref, num_ref, den_ref, win_ref, win_hbm, out_ref, win2_ref, sem):
    win = pltpu.make_async_copy(win_hbm.at[pl.ds(2 - 2 * core_ref[0], 2)], win2_ref, sem.at[0])
    win.start()
    zcols = norms_of(p_ref)
    for q in range(2):
        finish(0, p_ref, qf_ref, num_ref, den_ref, win_ref, out_ref, q, zcols)
    win.wait()


def second_kernel(core_ref, p_ref, qf_ref, num_ref, den_ref, win_ref, done_ref, out_hbm, out_ref, sems):
    core = core_ref[0]
    leaving = [leave(done_ref, out_hbm, core, q, sems.at[0]) for q in range(2)]
    zcols = norms_of(p_ref)
    for q in range(2):
        finish(1, p_ref, qf_ref, num_ref, den_ref, win_ref, out_ref, q, zcols)
        leaving.append(leave(out_ref, out_hbm, 1 - core, q, sems.at[1]))
    for copy in leaving:
        copy.wait()


def spec(kind=pltpu.VMEM):
    return pl.BlockSpec(memory_space=kind)


def call(kernel, ins, outs, scratch, flops, moved, name):
    made = pl.pallas_call(
        kernel,
        out_shape=[pltpu.HBM(o.shape, o.dtype) if k == HB else o for o, k in outs],
        in_specs=[spec(k) for k in ins],
        out_specs=[spec(k) for _, k in outs],
        scratch_shapes=scratch,
        compiler_params=pltpu.CompilerParams(vmem_limit_bytes=40 * 2**20),
        cost_estimate=pl.CostEstimate(flops=flops, bytes_accessed=moved, transcendentals=0),
        name=name,
    )
    return lambda *arrays: made(
        *(pltpu.with_memory_space_constraint(a, k) if k == HB else a for a, k in zip(arrays, ins, strict=True))
    )


def shape(*dims, dtype=F32):
    return jax.ShapeDtypeStruct(dims, dtype)


SM, VM, HB = pltpu.SMEM, pltpu.VMEM, pltpu.HBM
TURNED = pltpu.VMEM((256, ROWS), F32)
WIDE = pltpu.VMEM((QUADS, ROWS, 256), F32)
QF = (HEADS + QUADS, ROWS, LANES)
DENS = (ROWS, LANES)
BY_QUADS = (QUADS, ROWS, 256)
HALF_QF = (10, ROWS, LANES)
HALF = (2, ROWS, 256)


STATES = (PAIRS // 2, PAIR_ROWS, LANES)


def other_state(core, fk, v):
    return call(
        other_kernel, [SM, HB, HB],
        [(shape(*STATES), VM), (shape(256, ROWS), VM), (shape(ROWS, VALUES, dtype=BF16), VM)],
        [pltpu.VMEM((ROWS, 256), BF16), pltpu.SemaphoreType.DMA((2,))], 10**9, 5 * 10**6, "other",
    )(core, fk, v)


def chip_state(core, kt, v, got):
    return call(
        chip_kernel, [SM, VM, VM, VM], [(shape(*STATES), VM), (shape(*STATES), VM)], [], 10**9, 10**6, "chip"
    )(core, kt, v, got)


def spread(y, pieces, rows):
    flat = shape(PIECES * PROWS, LANES)
    return call(spread_kernel, [SM, VM, VM], [(flat, VM)], [], 10**6, 10**6, "spread")(
        y, pieces.reshape(flat.shape), rows.reshape(-1, LANES)
    )[0]


def intra(core, fq, fk, v, low, high):
    return call(
        intra_kernel, [SM] + [VM] * 5,
        [(shape(*QF, dtype=BF16), HB), (shape(*BY_QUADS), HB), (shape(*DENS), HB)],
        [TURNED, TURNED, pltpu.VMEM(QF, BF16), WIDE, pltpu.VMEM(DENS, F32), pltpu.SemaphoreType.DMA((4, 4))],
        2 * 10**9, 16 * 10**6, "intra",
    )(core, fq, fk, v, low, high)


def window(start, q, k, v, hk, hv):
    return call(
        window_kernel, [SM] + [VM] * 5, [(shape(*BY_QUADS), HB)], [WIDE, pltpu.SemaphoreType.DMA((4,))],
        2 * 10**9, 16 * 10**6, "window",
    )(start, q, k, v, hk, hv)[0]


OUT = (shape(ROWS, VALUES, dtype=BF16), HB)
OUT_SCRATCH = [pltpu.VMEM(HALF, BF16), pltpu.SemaphoreType.DMA((2,))]


def stage(core, qf, num, den, win):
    half = [(shape(*HALF_QF, dtype=BF16), VM), (shape(*HALF), VM)]
    return call(
        stage_kernel, [SM] + [HB] * 4, half + [(shape(*HALF), VM)] + half + [(shape(*DENS), VM)],
        [pltpu.SemaphoreType.DMA((8,))], 10**9, 10**7, "stage",
    )(core, qf, num, den, win)


def final_first(core, prior, qf, num, den, own_win, win):
    return call(
        first_kernel, [SM] + [VM] * 5 + [HB], [(shape(*HALF, dtype=BF16), VM), (shape(*HALF), VM)],
        [pltpu.SemaphoreType.DMA((1,))], 2 * 10**9, 10**6, "first",
    )(core, prior, qf, num, den, own_win, win)


def final_second(core, prior, qf, num, den, win, done):
    return call(
        second_kernel, [SM] + [VM] * 6, [(shape(ROWS, VALUES, dtype=BF16), HB)],
        [pltpu.VMEM(HALF, BF16), pltpu.SemaphoreType.DMA((2, 2))], 2 * 10**9, 10**6, "second",
    )(core, prior, qf, num, den, win, done)[0]


def exchange(array, axes):
    return lax.all_to_all(array, axes, split_axis=0, concat_axis=0, tiled=True)


def swap(array):
    return lax.ppermute(array, "c", [(0, 1), (1, 0)])


def scalar(value):
    return jnp.asarray(value, jnp.int32).reshape(1)


def after(first, *arrays):
    return lax.optimization_barrier((first, *arrays))


def body(fq, fk, v, wq, wk):
    core = scalar(lax.axis_index("c"))
    start = scalar(lax.axis_index(AXES))
    half = PAIRS // 2
    state, turned, held = other_state(core, fk, v)
    got = swap(state)
    own, chip = chip_state(core, turned, held, got)
    chip, own = after(chip.reshape(PIECES, *PIECE), own)
    pieces = exchange(chip, ("x", "z"))
    low, wk_out, v_out = after(swap(own), wk, v)
    count = lax.axis_size(AXES)
    pairs = [(i, i + 1) for i in range(count - 1)]
    hk = lax.ppermute(wk_out, AXES, pairs)
    hv = lax.ppermute(v_out, AXES, pairs)
    pieces, low = after(pieces, low)
    total = jnp.broadcast_to(jnp.sum(pieces, 0), (8, *PIECE))
    total, pieces, low, fq, fk = after(total, pieces, low, fq, fk)
    rows = exchange(total, "y")
    qf, num, den = intra(core, fq, fk, v, low, got)
    rows, qf, num, den = after(rows, qf, num, den)
    back = spread(scalar(lax.axis_index("y")), pieces, rows)
    back, wq = after(back.reshape(PIECES, *PIECE), wq)
    mine = exchange(back, ("x", "z"))
    win = window(start, wq, wk, v, hk, hv)
    staged = stage(core, qf, num, den, win)
    mine, *staged = after(mine, *staged)
    qf0, num0, win0, qf1, num1, den = staged
    mine = mine.reshape(half, PAIR_ROWS, LANES)
    other = swap(mine)
    done, win1 = final_first(core, mine, qf0, num0, den, win0, win)
    return final_second(core, other, qf1, num1, den, win1, done)


def solution(mesh):
    finer = Mesh(mesh.devices.reshape(8, 4, 8, 2), AXES)
    placed = P(AXES, None)
    return jax.shard_map(
        body, mesh=finer, in_specs=(placed,) * 5, out_specs=placed, check_vma=False
    )
```
